32 devices in a mesh: band: 4 (over x, core), col: 8 (over z, y).
Axes of the slice: x: 2, y: 2, z: 4, core: 2. Of those that a mesh axis runs over, the one named last changes fastest.
Arguments:
- adjoint_tend: bfloat16 [8, 40, 4, 5120], P('col', None, 'band'), may hold values from -6 to 6
- trajectory: bfloat16 [40, 4, 5120], P(None, 'band', 'col'), may hold values from -3 to 3
- coupling: bfloat16 [40, 40], replicated, may hold values from -1 to 1
- row_lat: int32 [4], P('band'), may hold values from 0 to 2559, as said below
- row_points: int32 [4], P('band'), may hold values from 20 to 5120, as said below
- wave_order: int32 [768], replicated, may hold values from 0 to 767, each once
Outputs:
- spectra: bfloat16 [8, 2, 40, 4, 768], P('col', None, None, None, 'band')
The draws below stay inside these ranges and needn't reach their ends.
Inputs may be any that keep to these rules, and one draw needn't show every extreme that they name: `row_lat`: latitude rows are counted from the north pole. `row_points`: the row of latitude index i has min(20 + 4 d, 5120) points, d = min(i, 2559 - i), placed at point indices 0 to that number minus one; the rest of the row slot is unused.
All inputs are finite; a program needn't handle non-finite values.
Results may differ from the reference program's by a relative error of at most 0.0055.
Values may be sent and summed in bfloat16 or wider, within the bound.
No kernel may reach another device: no remote copies, remote signals or barrier semaphores. Data moves between devices by JAX's collectives and lax.ppermute only.
A program may use at most 64 MiB of HBM per device.

```python
import math
import jax
import jax.numpy as jnp
from jax import lax

LEVELS = 8
COLUMN_VARS = 40
ROW_SLOTS = 5120
WAVES = 768
LATITUDES = 2560
ROWS = 4
MEMBERS = 8


def latitude_rows(key):
    picked = jax.random.randint(jax.random.fold_in(key, 11), (ROWS,), 0, LATITUDES)
    shuffled = jax.random.permutation(jax.random.fold_in(key, 12), ROWS)
    slots = jnp.arange(ROWS, dtype=jnp.int32)
    equator_slot = shuffled[0]
    south_slot = shuffled[1]
    north_slot = shuffled[2]
    values = jnp.where(slots == north_slot, 0, picked)
    values = jnp.where(slots == south_slot, LATITUDES - 1, values)
    values = jnp.where(slots == equator_slot, LATITUDES // 2, values)
    return values.astype(jnp.int32)


def draw_row_lat(key, part):
    return latitude_rows(key)


def draw_row_points(key, part):
    latitude = latitude_rows(key)
    distance = jnp.minimum(latitude, LATITUDES - 1 - latitude)
    return jnp.minimum(20 + 4 * distance, ROW_SLOTS).astype(jnp.int32)


def levels(own_key, dims, split, least, top_value):
    def one(dim, blocks):
        heights = jax.random.uniform(jax.random.fold_in(jax.random.fold_in(own_key, 6), dim), (blocks,), jnp.float32, least / len(split), top_value / len(split))
        return jnp.repeat(jnp.exp(heights), dims[dim] // blocks).reshape((-1,) + (1,) * (len(dims) - dim - 1))

    factor_of = one(*split[0])
    for cut in split[1:]:
        factor_of = factor_of * one(*cut)
    return factor_of


def centred(key, shape, deviation, most, split=(), held_as=jnp.bfloat16):
    entries = jax.random.normal(key, shape, jnp.float32) * deviation
    if len(split) > 0:
        entries = levels(key, shape, split, -0.22, 0.18) * entries
    return jnp.clip(entries, min=-most, max=most).astype(held_as)


def setup_inputs(seed: int = 0) -> dict:
    key_of = jax.random.split(jax.random.key(seed), 7)
    return {
        "adjoint_tend": centred(key_of[0], (MEMBERS, COLUMN_VARS, ROWS, ROW_SLOTS), 1.0, 6.0, ((0, 8), (2, 4))),
        "trajectory": centred(key_of[1], (COLUMN_VARS, ROWS, ROW_SLOTS), 0.5, 3.0, ((1, 4), (2, 8))),
        "coupling": centred(key_of[2], (COLUMN_VARS, COLUMN_VARS), COLUMN_VARS ** -0.5, 1.0),
        "row_lat": draw_row_lat(jax.random.fold_in(key_of[6], 71), 0),
        "row_points": draw_row_points(jax.random.fold_in(key_of[6], 71), 0),
        "wave_order": jax.random.permutation(key_of[5], WAVES).astype(jnp.int32),
    }


def latitude_factor(row_lat):
    ratio = (2.0 * row_lat.astype(jnp.float32) + 1.0) / LATITUDES
    return jnp.sin(0.5 * math.pi * (1.0 - ratio))

def grid_adjoint(tend_block, traj_block, coupling, coriolis, row_points, first_point):
    width = tend_block.shape[3]
    traj_wide = traj_block.astype(jnp.float32)
    coupling_wide = coupling.astype(jnp.float32)
    driven = jnp.einsum('ab,brp->arp', coupling_wide, traj_wide, precision=lax.Precision.HIGHEST)
    tend_wide = tend_block.astype(jnp.float32)
    weighted = tend_wide * (1.0 + traj_wide)[None]
    backed = jnp.einsum('ab,karp->kbrp', coupling_wide, weighted, precision=lax.Precision.HIGHEST)
    total = backed + tend_wide * driven[None]
    turning = coriolis[None, None, :, None]
    eastward = tend_wide[:, :LEVELS]
    northward = tend_wide[:, LEVELS:2 * LEVELS]
    total = jnp.concatenate([total[:, :LEVELS] - turning * northward, total[:, LEVELS:2 * LEVELS] + turning * eastward, total[:, 2 * LEVELS:]], axis=1)
    places = first_point + jnp.arange(width, dtype=jnp.int32)
    keep = places[None, :] < row_points[:, None]
    return jnp.where(keep[None, None], total, 0.0).astype(jnp.bfloat16)

def wave_table(points, waves, width):
    places = jnp.arange(width, dtype=jnp.int32)
    phase = places[:, None] * waves[None, :] % points
    angle = phase.astype(jnp.float32) * (2.0 * math.pi) / points.astype(jnp.float32)
    keep = (2 * waves < points)[None, :]
    cosine = jnp.where(keep, jnp.cos(angle), 0.0)
    sine = jnp.where(keep, -jnp.sin(angle), 0.0)
    return jnp.concatenate([cosine, sine], axis=1).astype(jnp.bfloat16)

def reference(adjoint_tend, trajectory, coupling, row_lat, row_points, wave_order):
    coriolis = latitude_factor(row_lat)

    def one_row(row_index):
        tend_row = lax.dynamic_slice_in_dim(adjoint_tend, row_index, 1, 2)
        traj_row = lax.dynamic_slice_in_dim(trajectory, row_index, 1, 1)
        turn_row = lax.dynamic_slice_in_dim(coriolis, row_index, 1, 0)
        count_row = lax.dynamic_slice_in_dim(row_points, row_index, 1, 0)
        grid = grid_adjoint(tend_row, traj_row, coupling, turn_row, count_row, 0)
        table = wave_table(count_row[0], wave_order, ROW_SLOTS)
        flat = grid.reshape(MEMBERS * COLUMN_VARS, ROW_SLOTS)
        coeffs = jnp.dot(flat.astype(jnp.float32), table.astype(jnp.float32), precision=lax.Precision.HIGHEST)
        coeffs = coeffs / jnp.sqrt(count_row[0].astype(jnp.float32))
        return coeffs.astype(jnp.bfloat16).reshape(MEMBERS, COLUMN_VARS, 2, WAVES)
    rows_out = lax.map(one_row, jnp.arange(ROWS, dtype=jnp.int32))
    return jnp.transpose(rows_out, (1, 3, 2, 0, 4))
```

```python
import functools
import math

import jax
import jax.numpy as jnp
from jax import lax
from jax.experimental import pallas as pl
from jax.experimental.pallas import tpu as pltpu
from jax.sharding import PartitionSpec as P

LEVELS = 8
LATITUDES = 2560
LANES = 128
SUB = 32


def partner(place, step, count):
    if count & (count - 1) == 0:
        return place ^ step
    return (place + step) % count


def source(place, step, count):
    if count & (count - 1) == 0:
        return place ^ step
    return (place - step) % count


def turn(places, waves, points):
    product = places * waves
    whole = jnp.floor(product * (1.0 / points) + 0.5)
    quarter = (product - whole * points) * 4.0 / points
    nearest = jnp.floor(quarter + 0.5)
    angle = (quarter - nearest) * (0.5 * math.pi)
    square = angle * angle
    sine = angle + angle * square * (
        -1.6666654611e-1 + square * (8.3321608736e-3 - square * 1.9515295891e-4)
    )
    cosine = (
        1.0
        - 0.5 * square
        + square
        * square
        * (4.166664568298827e-2 + square * (-1.388731625493765e-3 + square * 2.443315711809948e-5))
    )
    odd = jnp.abs(nearest) == 1.0
    first = jnp.where(odd, sine, cosine)
    second = jnp.where(odd, cosine, sine)
    first = jnp.where((nearest == 1.0) | (jnp.abs(nearest) >= 2.0), -first, first)
    second = jnp.where((nearest == -1.0) | (jnp.abs(nearest) >= 2.0), -second, second)
    return first, -second


def main_kernel(blocks, block, parts, *refs):
    index_ref, lat_ref, points_ref, waves_ref, mix_ref, tend_ref = refs[:6]
    traj_refs = refs[6 : 6 + blocks]
    out_refs = refs[6 + blocks : 6 + blocks + parts]
    table_ref, grid_ref = refs[6 + blocks + parts :]
    column_vars = tend_ref.shape[0]
    waves_total = waves_ref.shape[1]
    share = waves_total // parts
    count = points_ref[0]
    points = jnp.full((1, 1), count, jnp.int32).astype(jnp.float32)
    waves = waves_ref[...].astype(jnp.float32)

    coarse_rows = block // SUB
    coarse_pad = -(-coarse_rows // 8) * 8
    fine = lax.broadcasted_iota(jnp.int32, (SUB, 1), 0).astype(jnp.float32)
    coarse = lax.broadcasted_iota(jnp.int32, (coarse_pad, 1), 0).astype(jnp.float32) * SUB
    fine_cos, fine_sin = turn(fine, waves, points)
    coarse_cos, coarse_sin = turn(coarse, waves, points)
    for row in range(coarse_rows):
        here_cos = coarse_cos[row : row + 1]
        here_sin = coarse_sin[row : row + 1]
        rows = pl.ds(row * SUB, SUB)
        table_ref[rows, :waves_total] = (here_cos * fine_cos - here_sin * fine_sin).astype(
            jnp.bfloat16
        )
        table_ref[rows, waves_total:] = (here_cos * fine_sin + here_sin * fine_cos).astype(
            jnp.bfloat16
        )

    slot = lax.broadcasted_iota(jnp.int32, (blocks, 1), 0)
    first = jnp.zeros((blocks, 1), jnp.int32)
    for i in range(blocks):
        first = jnp.where(slot == i, index_ref[i] * block, first)
    phase_cos, phase_sin = turn(first.astype(jnp.float32), waves, points)
    scale = jnp.where(2.0 * waves < points, 1.0 / jnp.sqrt(points), 0.0)
    phase_cos = phase_cos * scale
    phase_sin = phase_sin * scale

    latitude = jnp.full((1, 1), lat_ref[0], jnp.int32).astype(jnp.float32)
    ratio = (2.0 * latitude + 1.0) / LATITUDES
    _, coriolis = turn(0.25 * (ratio - 1.0), jnp.ones((1, LANES), jnp.float32), 1.0)
    coriolis = coriolis[:, :1]

    mix = mix_ref[...]
    for i in range(blocks):
        start = index_ref[i] * block
        traj = traj_refs[i][...].astype(jnp.float32)
        tend = tend_ref[:, pl.ds(pl.multiple_of(start, LANES), block)].astype(jnp.float32)
        stacked = jnp.concatenate([traj, tend, tend * traj], axis=0).astype(jnp.bfloat16)
        mixed = jnp.dot(mix, stacked, preferred_element_type=jnp.float32)
        total = mixed[column_vars:] + tend * mixed[:column_vars]
        total = jnp.concatenate(
            [
                total[:LEVELS] - coriolis * tend[LEVELS : 2 * LEVELS],
                total[LEVELS : 2 * LEVELS] + coriolis * tend[:LEVELS],
                total[2 * LEVELS :],
            ],
            axis=0,
        )
        place = start + lax.broadcasted_iota(jnp.int32, (1, block), 1)
        grid_ref[pl.ds(i * column_vars, column_vars), :] = jnp.where(place < count, total, 0.0)

    flat = grid_ref[...].astype(jnp.bfloat16)
    reals = []
    imags = []
    width = math.gcd(waves_total, 256)
    for first_wave in range(0, waves_total, width):
        cols = slice(first_wave, first_wave + width)
        near_cos = jnp.dot(flat, table_ref[:, cols], preferred_element_type=jnp.float32)
        near_sin = jnp.dot(
            flat,
            table_ref[:, waves_total + first_wave : waves_total + first_wave + width],
            preferred_element_type=jnp.float32,
        )
        real = jnp.zeros((column_vars, width), jnp.float32)
        imag = jnp.zeros((column_vars, width), jnp.float32)
        for i in range(blocks):
            rows = slice(i * column_vars, (i + 1) * column_vars)
            far_cos = phase_cos[i : i + 1, cols]
            far_sin = phase_sin[i : i + 1, cols]
            real = real + (far_cos * near_cos[rows] - far_sin * near_sin[rows])
            imag = imag + (far_cos * near_sin[rows] + far_sin * near_cos[rows])
        reals.append(real)
        imags.append(imag)
    both = jnp.concatenate(
        [jnp.concatenate(reals, axis=1), jnp.concatenate(imags, axis=1)], axis=0
    )
    for k in range(parts):
        out_refs[k][...] = both[:, k * share : (k + 1) * share].astype(jnp.bfloat16)


def place_kernel(parts, *refs):
    target_ref = refs[0]
    in_refs = refs[1 : 1 + parts]
    out_ref = refs[1 + parts]
    total = target_ref.shape[0]
    column_vars = total // parts
    choose = (
        target_ref[...] == lax.broadcasted_iota(jnp.int32, (total, total), 1)
    ).astype(jnp.bfloat16)
    wide = [ref[...].astype(jnp.float32) for ref in in_refs]
    for half in range(2):
        rows = slice(half * column_vars, (half + 1) * column_vars)
        stacked = jnp.concatenate([w[rows] for w in wide], axis=0).astype(jnp.bfloat16)
        out_ref[half] = jnp.dot(
            choose, stacked, preferred_element_type=jnp.float32
        ).astype(jnp.bfloat16)


VMEM_SPEC = pl.BlockSpec(memory_space=pltpu.VMEM)
SMEM_SPEC = pl.BlockSpec(memory_space=pltpu.SMEM)


def body(cols, bands, adjoint_tend, trajectory, coupling, row_lat, row_points, wave_order):
    column_vars = adjoint_tend.shape[1]
    width = adjoint_tend.shape[3]
    own = trajectory.shape[2]
    waves_total = wave_order.shape[0]
    share = waves_total // bands
    my_col = lax.axis_index("col")
    my_band = lax.axis_index("band")
    tend = adjoint_tend.reshape(column_vars, width)
    traj = trajectory.reshape(column_vars, own)

    if own % LANES == 0:
        block = own
        pieces = [traj]
        indices = [my_col]
        for step in range(1, cols):
            pairs = [(i, partner(i, step, cols)) for i in range(cols)]
            pieces.append(lax.ppermute(traj, "col", pairs))
            indices.append(source(my_col, step, cols))
        indices = jnp.stack(indices)
    else:
        block = width // 8
        whole = lax.all_gather(traj, "col", axis=1, tiled=True)
        pieces = [whole[:, i * block : (i + 1) * block] for i in range(8)]
        indices = jnp.arange(8, dtype=jnp.int32)
    blocks = len(pieces)

    waves = jnp.concatenate(
        [
            lax.dynamic_slice_in_dim(wave_order, partner(my_band, k, bands) * share, share)
            for k in range(bands)
        ]
    ).reshape(1, waves_total)
    none = jnp.zeros_like(coupling)
    mix = jnp.concatenate(
        [
            jnp.concatenate([coupling, none, none], axis=1),
            jnp.concatenate([none, coupling.T, coupling.T], axis=1),
        ],
        axis=0,
    )
    flops = 2 * column_vars * width * 2 * waves_total
    parts = pl.pallas_call(
        functools.partial(main_kernel, blocks, block, bands),
        out_shape=[jax.ShapeDtypeStruct((2 * column_vars, share), jnp.bfloat16)] * bands,
        in_specs=[SMEM_SPEC] * 3 + [VMEM_SPEC] * (3 + blocks),
        out_specs=[VMEM_SPEC] * bands,
        scratch_shapes=[
            pltpu.VMEM((block, 2 * waves_total), jnp.bfloat16),
            pltpu.VMEM((blocks * column_vars, block), jnp.float32),
        ],
        compiler_params=pltpu.CompilerParams(vmem_limit_bytes=40 * 1024 * 1024),
        cost_estimate=pl.CostEstimate(
            flops=flops, bytes_accessed=4 * column_vars * width, transcendentals=0
        ),
        name="column_and_waves",
    )(indices, row_lat, row_points, waves, mix, tend, *pieces)

    arrived = [parts[0]]
    for step in range(1, bands):
        pairs = [(i, partner(i, step, bands)) for i in range(bands)]
        arrived.append(lax.ppermute(parts[step], "band", pairs))
    row = jnp.arange(column_vars * bands, dtype=jnp.int32)
    variable, slot = row // bands, row % bands
    step_of = slot ^ my_band if bands & (bands - 1) == 0 else (my_band - slot) % bands
    target = (step_of * column_vars + variable).reshape(-1, 1)
    spectra = pl.pallas_call(
        functools.partial(place_kernel, bands),
        out_shape=jax.ShapeDtypeStruct((2, column_vars * bands, share), jnp.bfloat16),
        in_specs=[VMEM_SPEC] * (1 + bands),
        out_specs=VMEM_SPEC,
        name="row_slots",
    )(target, *arrived)
    return spectra.reshape(1, 2, column_vars, bands, share)


def solution(mesh):
    return jax.shard_map(
        functools.partial(body, mesh.shape["col"], mesh.shape["band"]),
        mesh=mesh,
        in_specs=(
            P("col", None, "band", None),
            P(None, "band", "col"),
            P(),
            P("band"),
            P("band"),
            P(),
        ),
        out_specs=P("col", None, None, None, "band"),
        check_vma=False,
    )
```

```python
import functools
import math

import jax
import jax.numpy as jnp
from jax import lax
from jax.experimental import pallas as pl
from jax.experimental.pallas import tpu as pltpu
from jax.sharding import PartitionSpec as P

LEVELS = 8
LATITUDES = 2560
LANES = 128
SUB = 32


def partner(place, step, count):
    if count & (count - 1) == 0:
        return place ^ step
    return (place + step) % count


def source(place, step, count):
    if count & (count - 1) == 0:
        return place ^ step
    return (place - step) % count


def turn(places, waves, points):
    product = places * waves
    whole = jnp.floor(product * (1.0 / points) + 0.5)
    quarter = (product - whole * points) * 4.0 / points
    nearest = jnp.floor(quarter + 0.5)
    angle = (quarter - nearest) * (0.5 * math.pi)
    square = angle * angle
    sine = angle + angle * square * (
        -1.6666654611e-1 + square * (8.3321608736e-3 - square * 1.9515295891e-4)
    )
    cosine = (
        1.0
        - 0.5 * square
        + square
        * square
        * (4.166664568298827e-2 + square * (-1.388731625493765e-3 + square * 2.443315711809948e-5))
    )
    odd = jnp.abs(nearest) == 1.0
    first = jnp.where(odd, sine, cosine)
    second = jnp.where(odd, cosine, sine)
    first = jnp.where((nearest == 1.0) | (jnp.abs(nearest) >= 2.0), -first, first)
    second = jnp.where((nearest == -1.0) | (jnp.abs(nearest) >= 2.0), -second, second)
    return first, -second


def tables_kernel(
    blocks, block, index_of, lat_ref, waves_hbm, coupling_hbm, tend_hbm, traj_hbm, *refs
):
    table_ref, phase_ref, mix_ref, kept_ref, own_ref, coriolis_ref = refs[:6]
    waves_ref, coupling_ref, tend_ref, sems = refs[6:]
    copies = [
        pltpu.make_async_copy(source_ref, target_ref, sems.at[i])
        for i, (source_ref, target_ref) in enumerate(
            [
                (waves_hbm, waves_ref),
                (coupling_hbm, coupling_ref),
                (tend_hbm, tend_ref),
                (traj_hbm, own_ref),
            ]
        )
    ]
    for copy in copies:
        copy.start()
    index = lat_ref[0]
    count = jnp.minimum(20 + 4 * jnp.minimum(index, LATITUDES - 1 - index), tend_ref.shape[1])
    copies[0].wait()
    waves_total = waves_ref.shape[0]
    points = jnp.full((1, 1), count, jnp.int32).astype(jnp.float32)
    waves = waves_ref[...].reshape(1, waves_total).astype(jnp.float32)

    coarse_rows = block // SUB
    coarse_pad = -(-coarse_rows // 8) * 8
    fine = lax.broadcasted_iota(jnp.int32, (SUB, 1), 0).astype(jnp.float32)
    coarse = lax.broadcasted_iota(jnp.int32, (coarse_pad, 1), 0).astype(jnp.float32) * SUB
    fine_cos, fine_sin = turn(fine, waves, points)
    coarse_cos, coarse_sin = turn(coarse, waves, points)
    for row in range(coarse_rows):
        here_cos = coarse_cos[row : row + 1]
        here_sin = coarse_sin[row : row + 1]
        rows = pl.ds(row * SUB, SUB)
        table_ref[rows, :waves_total] = (here_cos * fine_cos - here_sin * fine_sin).astype(
            jnp.bfloat16
        )
        table_ref[rows, waves_total:] = (here_cos * fine_sin + here_sin * fine_cos).astype(
            jnp.bfloat16
        )

    slot = lax.broadcasted_iota(jnp.int32, (blocks, 1), 0)
    first = jnp.zeros((blocks, 1), jnp.int32)
    for i, of_row in enumerate(index_of()):
        first = jnp.where(slot == i, of_row * block, first)
    phase_cos, phase_sin = turn(first.astype(jnp.float32), waves, points)
    scale = jnp.where(2.0 * waves < points, 1.0 / jnp.sqrt(points), 0.0)
    phase_ref[0] = phase_cos * scale
    phase_ref[1] = phase_sin * scale

    latitude = jnp.full((1, LANES), index, jnp.int32).astype(jnp.float32)
    ratio = (2.0 * latitude + 1.0) / LATITUDES
    coriolis_ref[...] = turn(0.25 * (ratio - 1.0), jnp.ones((1, LANES), jnp.float32), 1.0)[1]

    copies[1].wait()
    column_vars = coupling_ref.shape[0]
    coupling = coupling_ref[...]
    row = lax.broadcasted_iota(jnp.int32, (column_vars, 3 * column_vars), 0)
    col = lax.broadcasted_iota(jnp.int32, (column_vars, 3 * column_vars), 1)
    near = (col == row).astype(jnp.bfloat16)
    far = ((col == row + column_vars) | (col == row + 2 * column_vars)).astype(jnp.bfloat16)
    mix_ref[...] = jnp.concatenate(
        [
            jnp.dot(coupling, near, preferred_element_type=jnp.float32),
            lax.dot_general(
                coupling, far, (((0,), (0,)), ((), ())), preferred_element_type=jnp.float32
            ),
        ],
        axis=0,
    ).astype(jnp.bfloat16)

    copies[2].wait()
    for i in range(blocks):
        cols = slice(i * block, (i + 1) * block)
        place = i * block + lax.broadcasted_iota(jnp.int32, (1, block), 1)
        kept_ref[:, cols] = jnp.where(
            place < count, tend_ref[:, cols].astype(jnp.float32), 0.0
        ).astype(jnp.bfloat16)
    copies[3].wait()


def main_kernel(blocks, block, parts, index_of, *refs):
    coriolis_ref, mix_ref, table_ref, phase_ref, tend_ref = refs[:5]
    traj_refs = refs[5 : 5 + blocks]
    out_refs = refs[5 + blocks : 5 + blocks + parts]
    grid_ref = refs[5 + blocks + parts]
    column_vars = tend_ref.shape[0]
    waves_total = phase_ref.shape[2]
    share = waves_total // parts

    coriolis = coriolis_ref[:, :1]
    mix = mix_ref[...]
    for i, index in enumerate(index_of()):
        start = pl.multiple_of(index * block, LANES)
        traj = traj_refs[i][...].astype(jnp.float32)
        tend = tend_ref[:, pl.ds(start, block)].astype(jnp.float32)
        stacked = jnp.concatenate([traj, tend, tend * traj], axis=0).astype(jnp.bfloat16)
        mixed = jnp.dot(mix, stacked, preferred_element_type=jnp.float32)
        total = mixed[column_vars:] + tend * mixed[:column_vars]
        grid_ref[pl.ds(i * column_vars, column_vars), :] = jnp.concatenate(
            [
                total[:LEVELS] - coriolis * tend[LEVELS : 2 * LEVELS],
                total[LEVELS : 2 * LEVELS] + coriolis * tend[:LEVELS],
                total[2 * LEVELS :],
            ],
            axis=0,
        )

    flat = grid_ref[...].astype(jnp.bfloat16)
    reals = []
    imags = []
    width = math.gcd(waves_total, 256)
    for first_wave in range(0, waves_total, width):
        cols = slice(first_wave, first_wave + width)
        near_cos = jnp.dot(flat, table_ref[:, cols], preferred_element_type=jnp.float32)
        near_sin = jnp.dot(
            flat,
            table_ref[:, waves_total + first_wave : waves_total + first_wave + width],
            preferred_element_type=jnp.float32,
        )
        real = jnp.zeros((column_vars, width), jnp.float32)
        imag = jnp.zeros((column_vars, width), jnp.float32)
        for i in range(blocks):
            rows = slice(i * column_vars, (i + 1) * column_vars)
            far_cos = phase_ref[0, i : i + 1, cols]
            far_sin = phase_ref[1, i : i + 1, cols]
            real = real + (far_cos * near_cos[rows] - far_sin * near_sin[rows])
            imag = imag + (far_cos * near_sin[rows] + far_sin * near_cos[rows])
        reals.append(real)
        imags.append(imag)
    both = jnp.concatenate(
        [jnp.concatenate(reals, axis=1), jnp.concatenate(imags, axis=1)], axis=0
    )
    shares = [both[:, d * share : (d + 1) * share] for d in range(parts)]
    my_band = lax.axis_index("band")
    for k in range(parts):
        goal = partner(my_band, k, parts)
        chosen = shares[0]
        for d in range(1, parts):
            chosen = jnp.where(goal == d, shares[d], chosen)
        out_refs[k][...] = chosen.astype(jnp.bfloat16)


def place_kernel(parts, *refs):
    in_refs = refs[:parts]
    out_ref = refs[parts]
    column_vars = out_ref.shape[2]
    share = out_ref.shape[4]
    total = parts * column_vars
    row = lax.broadcasted_iota(jnp.int32, (total, 1), 0)
    variable = jnp.floor((row.astype(jnp.float32) + 0.5) * (1.0 / parts)).astype(jnp.int32)
    slot = row - variable * parts
    if parts & (parts - 1) == 0:
        step = slot ^ lax.axis_index("band")
    else:
        step = lax.axis_index("band") - slot
        step = jnp.where(step < 0, step + parts, step)
    target = step * column_vars + variable
    choose = (target == lax.broadcasted_iota(jnp.int32, (total, total), 1)).astype(jnp.bfloat16)
    wide = [ref[...].astype(jnp.float32) for ref in in_refs]
    for half in range(2):
        rows = slice(half * column_vars, (half + 1) * column_vars)
        stacked = jnp.concatenate([w[rows] for w in wide], axis=0).astype(jnp.bfloat16)
        placed = jnp.dot(choose, stacked, preferred_element_type=jnp.float32)
        out_ref[0, half] = placed.reshape(column_vars, parts, share).astype(jnp.bfloat16)


VMEM_SPEC = pl.BlockSpec(memory_space=pltpu.VMEM)
SMEM_SPEC = pl.BlockSpec(memory_space=pltpu.SMEM)
HBM_SPEC = pl.BlockSpec(memory_space=pltpu.HBM)


def body(cols, bands, adjoint_tend, trajectory, coupling, row_lat, row_points, wave_order):
    column_vars = adjoint_tend.shape[1]
    width = adjoint_tend.shape[3]
    own = trajectory.shape[2]
    waves_total = wave_order.shape[0]
    share = waves_total // bands
    tend = adjoint_tend.reshape(column_vars, width)
    traj = trajectory.reshape(column_vars, own)

    inner = 2 if cols % 2 == 0 else 1
    outer = cols // inner
    direct = own % LANES == 0
    blocks = cols if direct else 8
    block = width // blocks

    def index_of():
        if not direct:
            return list(range(blocks))
        my_col = lax.axis_index("col")
        far, near = my_col // inner, my_col % inner
        indices = [source(far, step, outer) * inner + near for step in range(outer)]
        return indices + [index ^ 1 for index in indices] if inner == 2 else indices

    operands = [wave_order, coupling, tend, traj]
    table, phase, mix, kept, own_piece, coriolis = pl.pallas_call(
        functools.partial(tables_kernel, blocks, block, index_of),
        out_shape=[
            jax.ShapeDtypeStruct((block, 2 * waves_total), jnp.bfloat16),
            jax.ShapeDtypeStruct((2, blocks, waves_total), jnp.float32),
            jax.ShapeDtypeStruct((2 * column_vars, 3 * column_vars), jnp.bfloat16),
            jax.ShapeDtypeStruct((column_vars, width), jnp.bfloat16),
            jax.ShapeDtypeStruct((column_vars, own), jnp.bfloat16),
            jax.ShapeDtypeStruct((1, LANES), jnp.float32),
        ],
        in_specs=[SMEM_SPEC] + [HBM_SPEC] * len(operands),
        out_specs=[VMEM_SPEC] * 6,
        scratch_shapes=[
            pltpu.VMEM((waves_total,), jnp.int32),
            pltpu.VMEM((column_vars, column_vars), jnp.bfloat16),
            pltpu.VMEM((column_vars, width), jnp.bfloat16),
            pltpu.SemaphoreType.DMA((len(operands),)),
        ],
        compiler_params=pltpu.CompilerParams(vmem_limit_bytes=16 * 1024 * 1024),
        cost_estimate=pl.CostEstimate(
            flops=1024 * column_vars * width, bytes_accessed=4 * column_vars * width, transcendentals=0
        ),
        name="tables",
    )(row_lat, *[pltpu.with_memory_space_constraint(x, pltpu.HBM) for x in operands])

    if direct:
        places = [(i // inner, i % inner) for i in range(cols)]
        arrived = []
        for step in range(1, outer):
            pairs = [(f * inner + n, partner(f, step, outer) * inner + n) for f, n in places]
            arrived.append(lax.ppermute(traj, "col", pairs))
        if inner == 2:
            pairs = [(i, i ^ 1) for i in range(cols)]
            passed = [lax.optimization_barrier((piece, coriolis))[0] for piece in arrived]
            arrived += [lax.ppermute(piece, "col", pairs) for piece in [traj] + passed]
    else:
        whole = lax.all_gather(traj, "col", axis=1, tiled=True)
        arrived = [whole[:, i * block : (i + 1) * block] for i in range(8)]

    pieces = [own_piece] + arrived if direct else arrived
    parts = pl.pallas_call(
        functools.partial(main_kernel, blocks, block, bands, index_of),
        out_shape=[jax.ShapeDtypeStruct((2 * column_vars, share), jnp.bfloat16)] * bands,
        in_specs=[VMEM_SPEC] * (5 + blocks),
        out_specs=[VMEM_SPEC] * bands,
        scratch_shapes=[pltpu.VMEM((blocks * column_vars, block), jnp.float32)],
        compiler_params=pltpu.CompilerParams(vmem_limit_bytes=24 * 1024 * 1024),
        cost_estimate=pl.CostEstimate(
            flops=4 * column_vars * width * waves_total,
            bytes_accessed=4 * column_vars * width,
            transcendentals=0,
        ),
        name="column_and_waves",
    )(coriolis, mix, table, phase, kept, *pieces)

    ready = [parts[0]]
    for step in range(1, bands):
        pairs = [(i, partner(i, step, bands)) for i in range(bands)]
        ready.append(lax.ppermute(parts[step], "band", pairs))
    return pl.pallas_call(
        functools.partial(place_kernel, bands),
        out_shape=jax.ShapeDtypeStruct((1, 2, column_vars, bands, share), jnp.bfloat16),
        in_specs=[VMEM_SPEC] * bands,
        out_specs=VMEM_SPEC,
        compiler_params=pltpu.CompilerParams(vmem_limit_bytes=16 * 1024 * 1024),
        name="row_slots",
    )(*ready)


def solution(mesh):
    return jax.shard_map(
        functools.partial(body, mesh.shape["col"], mesh.shape["band"]),
        mesh=mesh,
        in_specs=(
            P("col", None, "band", None),
            P(None, "band", "col"),
            P(),
            P("band"),
            P("band"),
            P(),
        ),
        out_specs=P("col", None, None, None, "band"),
        check_vma=False,
    )
```

```python
import functools
import math

import jax
import jax.numpy as jnp
from jax import lax
from jax.experimental import pallas as pl
from jax.experimental.pallas import tpu as pltpu
from jax.sharding import PartitionSpec as P

LEVELS = 8
LATITUDES = 2560
LANES = 128
SUB = 32


def partner(place, step, count):
    if count & (count - 1) == 0:
        return place ^ step
    return (place + step) % count


def source(place, step, count):
    if count & (count - 1) == 0:
        return place ^ step
    return (place - step) % count


def turn(places, waves, points):
    product = places * waves
    whole = jnp.floor(product * (1.0 / points) + 0.5)
    quarter = (product - whole * points) * 4.0 / points
    nearest = jnp.floor(quarter + 0.5)
    angle = (quarter - nearest) * (0.5 * math.pi)
    square = angle * angle
    sine = angle + angle * square * (
        -1.6666654611e-1 + square * (8.3321608736e-3 - square * 1.9515295891e-4)
    )
    cosine = (
        1.0
        - 0.5 * square
        + square
        * square
        * (4.166664568298827e-2 + square * (-1.388731625493765e-3 + square * 2.443315711809948e-5))
    )
    odd = jnp.abs(nearest) == 1.0
    first = jnp.where(odd, sine, cosine)
    second = jnp.where(odd, cosine, sine)
    first = jnp.where((nearest == 1.0) | (jnp.abs(nearest) >= 2.0), -first, first)
    second = jnp.where((nearest == -1.0) | (jnp.abs(nearest) >= 2.0), -second, second)
    return first, -second


def tables_kernel(
    blocks, block, held, index_of, lat_ref, waves_hbm, coupling_hbm, tend_hbm, traj_hbm, *refs
):
    far_table_ref, own_table_ref, phase_ref, mix_ref, kept_ref, own_ref, coriolis_ref = refs[:7]
    waves_ref, coupling_ref, tend_ref, sems = refs[7:]
    copies = [
        pltpu.make_async_copy(source_ref, target_ref, sems.at[i])
        for i, (source_ref, target_ref) in enumerate(
            [
                (waves_hbm, waves_ref),
                (coupling_hbm, coupling_ref),
                (tend_hbm, tend_ref),
                (traj_hbm, own_ref),
            ]
        )
    ]
    for copy in copies:
        copy.start()
    index = lat_ref[0]
    count = jnp.minimum(20 + 4 * jnp.minimum(index, LATITUDES - 1 - index), tend_ref.shape[1])
    copies[0].wait()
    waves_total = waves_ref.shape[0]
    points = jnp.full((1, 1), count, jnp.int32).astype(jnp.float32)
    waves = waves_ref[...].reshape(1, waves_total).astype(jnp.float32)
    bands = len(held)
    share = waves_total // bands
    shares = [waves[:, d * share : (d + 1) * share] for d in range(bands)]
    my_band = lax.axis_index("band")
    ordered = []
    for step in held:
        goal = partner(my_band, step, bands)
        chosen = shares[0]
        for d in range(1, bands):
            chosen = jnp.where(goal == d, shares[d], chosen)
        ordered.append(chosen)
    waves = jnp.concatenate(ordered, axis=1)

    coarse_rows = block // SUB
    coarse_pad = -(-coarse_rows // 8) * 8
    fine = lax.broadcasted_iota(jnp.int32, (SUB, 1), 0).astype(jnp.float32)
    coarse = lax.broadcasted_iota(jnp.int32, (coarse_pad, 1), 0).astype(jnp.float32) * SUB
    fine_cos, fine_sin = turn(fine, waves, points)
    coarse_cos, coarse_sin = turn(coarse, waves, points)
    for row in range(coarse_rows):
        here_cos = coarse_cos[row : row + 1]
        here_sin = coarse_sin[row : row + 1]
        rows = pl.ds(row * SUB, SUB)
        table_cos = (here_cos * fine_cos - here_sin * fine_sin).astype(jnp.bfloat16)
        table_sin = (here_cos * fine_sin + here_sin * fine_cos).astype(jnp.bfloat16)
        far = waves_total - share
        far_table_ref[rows, :far] = table_cos[:, :far]
        far_table_ref[rows, far:] = table_sin[:, :far]
        own_table_ref[rows, :share] = table_cos[:, far:]
        own_table_ref[rows, share:] = table_sin[:, far:]

    slot = lax.broadcasted_iota(jnp.int32, (blocks, 1), 0)
    first = jnp.zeros((blocks, 1), jnp.int32)
    for i, of_row in enumerate(index_of()):
        first = jnp.where(slot == i, of_row * block, first)
    phase_cos, phase_sin = turn(first.astype(jnp.float32), waves, points)
    scale = jnp.where(2.0 * waves < points, 1.0 / jnp.sqrt(points), 0.0)
    phase_ref[0] = phase_cos * scale
    phase_ref[1] = phase_sin * scale

    latitude = jnp.full((1, LANES), index, jnp.int32).astype(jnp.float32)
    ratio = (2.0 * latitude + 1.0) / LATITUDES
    coriolis_ref[...] = turn(0.25 * (ratio - 1.0), jnp.ones((1, LANES), jnp.float32), 1.0)[1]

    copies[1].wait()
    column_vars = coupling_ref.shape[0]
    coupling = coupling_ref[...]
    row = lax.broadcasted_iota(jnp.int32, (column_vars, 3 * column_vars), 0)
    col = lax.broadcasted_iota(jnp.int32, (column_vars, 3 * column_vars), 1)
    near = (col == row).astype(jnp.bfloat16)
    far = ((col == row + column_vars) | (col == row + 2 * column_vars)).astype(jnp.bfloat16)
    mix_ref[...] = jnp.concatenate(
        [
            jnp.dot(coupling, near, preferred_element_type=jnp.float32),
            lax.dot_general(
                coupling, far, (((0,), (0,)), ((), ())), preferred_element_type=jnp.float32
            ),
        ],
        axis=0,
    ).astype(jnp.bfloat16)

    copies[2].wait()
    for i in range(blocks):
        cols = slice(i * block, (i + 1) * block)
        place = i * block + lax.broadcasted_iota(jnp.int32, (1, block), 1)
        kept_ref[:, cols] = jnp.where(
            place < count, tend_ref[:, cols].astype(jnp.float32), 0.0
        ).astype(jnp.bfloat16)
    copies[3].wait()


def transform(flat, table_ref, phase_ref, first_wave, out_refs):
    column_vars = out_refs[0].shape[0] // 2
    blocks = flat.shape[0] // column_vars
    wide = table_ref.shape[1]
    waves = wide // 2
    share = out_refs[0].shape[1]
    near = jnp.concatenate(
        [
            jnp.dot(flat, table_ref[:, i : min(i + 256, wide)], preferred_element_type=jnp.float32)
            for i in range(0, wide, 256)
        ],
        axis=1,
    )
    real = jnp.zeros((column_vars, waves), jnp.float32)
    imag = jnp.zeros((column_vars, waves), jnp.float32)
    for i in range(blocks):
        rows = slice(i * column_vars, (i + 1) * column_vars)
        near_cos, near_sin = near[rows, :waves], near[rows, waves:]
        far_cos = phase_ref[0, i : i + 1, first_wave : first_wave + waves]
        far_sin = phase_ref[1, i : i + 1, first_wave : first_wave + waves]
        real = real + (far_cos * near_cos - far_sin * near_sin)
        imag = imag + (far_cos * near_sin + far_sin * near_cos)
    both = jnp.concatenate([real, imag], axis=0)
    for k, out_ref in enumerate(out_refs):
        out_ref[...] = both[:, k * share : (k + 1) * share].astype(jnp.bfloat16)


def main_kernel(blocks, block, index_of, *refs):
    coriolis_ref, mix_ref, table_ref, phase_ref, tend_ref = refs[:5]
    traj_refs = refs[5 : 5 + blocks]
    flat_ref = refs[5 + blocks]
    out_refs = refs[6 + blocks : -1]
    grid_ref = refs[-1]
    column_vars = tend_ref.shape[0]
    coriolis = coriolis_ref[:, :1]
    mix = mix_ref[...]
    for i, index in enumerate(index_of()):
        start = pl.multiple_of(index * block, LANES)
        traj = traj_refs[i][...].astype(jnp.float32)
        tend = tend_ref[:, pl.ds(start, block)].astype(jnp.float32)
        stacked = jnp.concatenate([traj, tend, tend * traj], axis=0).astype(jnp.bfloat16)
        mixed = jnp.dot(mix, stacked, preferred_element_type=jnp.float32)
        total = mixed[column_vars:] + tend * mixed[:column_vars]
        grid_ref[pl.ds(i * column_vars, column_vars), :] = jnp.concatenate(
            [
                total[:LEVELS] - coriolis * tend[LEVELS : 2 * LEVELS],
                total[LEVELS : 2 * LEVELS] + coriolis * tend[:LEVELS],
                total[2 * LEVELS :],
            ],
            axis=0,
        )
    flat = grid_ref[...].astype(jnp.bfloat16)
    flat_ref[...] = flat
    transform(flat, table_ref, phase_ref, 0, out_refs)


def own_kernel(flat_ref, table_ref, phase_ref, out_ref):
    first_wave = phase_ref.shape[2] - out_ref.shape[1]
    transform(flat_ref[...], table_ref, phase_ref, first_wave, [out_ref])


def place_kernel(held, *refs):
    parts = len(held)
    in_refs = refs[:parts]
    out_ref = refs[parts]
    column_vars = out_ref.shape[2]
    share = out_ref.shape[4]
    total = parts * column_vars
    row = lax.broadcasted_iota(jnp.int32, (total, 1), 0)
    variable = jnp.floor((row.astype(jnp.float32) + 0.5) * (1.0 / parts)).astype(jnp.int32)
    slot = row - variable * parts
    if parts & (parts - 1) == 0:
        step = slot ^ lax.axis_index("band")
    else:
        step = lax.axis_index("band") - slot
        step = jnp.where(step < 0, step + parts, step)
    target = variable
    for position, which in enumerate(held):
        target = jnp.where(step == which, target + position * column_vars, target)
    choose = (target == lax.broadcasted_iota(jnp.int32, (total, total), 1)).astype(jnp.bfloat16)
    wide = [ref[...].astype(jnp.float32) for ref in in_refs]
    for half in range(2):
        rows = slice(half * column_vars, (half + 1) * column_vars)
        stacked = jnp.concatenate([w[rows] for w in wide], axis=0).astype(jnp.bfloat16)
        placed = jnp.dot(choose, stacked, preferred_element_type=jnp.float32)
        out_ref[0, half] = placed.reshape(column_vars, parts, share).astype(jnp.bfloat16)


VMEM_SPEC = pl.BlockSpec(memory_space=pltpu.VMEM)
SMEM_SPEC = pl.BlockSpec(memory_space=pltpu.SMEM)
HBM_SPEC = pl.BlockSpec(memory_space=pltpu.HBM)


def body(cols, bands, adjoint_tend, trajectory, coupling, row_lat, row_points, wave_order):
    column_vars = adjoint_tend.shape[1]
    width = adjoint_tend.shape[3]
    own = trajectory.shape[2]
    waves_total = wave_order.shape[0]
    share = waves_total // bands
    tend = adjoint_tend.reshape(column_vars, width)
    traj = trajectory.reshape(column_vars, own)

    inner = 2 if cols % 2 == 0 else 1
    outer = cols // inner
    direct = own % LANES == 0
    order = sorted(range(1, outer), key=lambda step: (step > 2, -step))
    moves = [(step, 0) for step in order]
    if inner == 2:
        moves += [(0, 1)] + [(step, 1) for step in order]
    blocks = cols if direct else 8
    held = list(reversed(range(bands)))
    block = width // blocks

    def index_of():
        if not direct:
            return list(range(blocks))
        my_col = lax.axis_index("col")
        far, near = my_col // inner, my_col % inner
        return [my_col] + [
            source(far, step, outer) * inner + (near ^ turned) for step, turned in moves
        ]

    operands = [wave_order, coupling, tend, traj]
    far_table, own_table, phase, mix, kept, own_piece, coriolis = pl.pallas_call(
        functools.partial(tables_kernel, blocks, block, held, index_of),
        out_shape=[
            jax.ShapeDtypeStruct((block, 2 * (waves_total - share)), jnp.bfloat16),
            jax.ShapeDtypeStruct((block, 2 * share), jnp.bfloat16),
            jax.ShapeDtypeStruct((2, blocks, waves_total), jnp.float32),
            jax.ShapeDtypeStruct((2 * column_vars, 3 * column_vars), jnp.bfloat16),
            jax.ShapeDtypeStruct((column_vars, width), jnp.bfloat16),
            jax.ShapeDtypeStruct((column_vars, own), jnp.bfloat16),
            jax.ShapeDtypeStruct((1, LANES), jnp.float32),
        ],
        in_specs=[SMEM_SPEC] + [HBM_SPEC] * len(operands),
        out_specs=[VMEM_SPEC] * 7,
        scratch_shapes=[
            pltpu.VMEM((waves_total,), jnp.int32),
            pltpu.VMEM((column_vars, column_vars), jnp.bfloat16),
            pltpu.VMEM((column_vars, width), jnp.bfloat16),
            pltpu.SemaphoreType.DMA((len(operands),)),
        ],
        compiler_params=pltpu.CompilerParams(vmem_limit_bytes=16 * 1024 * 1024),
        cost_estimate=pl.CostEstimate(
            flops=1024 * column_vars * width, bytes_accessed=4 * column_vars * width, transcendentals=0
        ),
        name="tables",
    )(row_lat, *[pltpu.with_memory_space_constraint(x, pltpu.HBM) for x in operands])

    if direct:
        places = [(i // inner, i % inner) for i in range(cols)]
        moved = {}
        for step, turned in moves:
            if turned and step > 1:
                pairs = [(i, i ^ 1) for i in range(cols)]
                moved[step, turned] = lax.ppermute(moved[step, 0], "col", pairs)
            else:
                pairs = [
                    (f * inner + n, partner(f, step, outer) * inner + (n ^ turned)) for f, n in places
                ]
                moved[step, turned] = lax.ppermute(traj, "col", pairs)
        arrived = [moved[move] for move in moves]
    else:
        whole = lax.all_gather(traj, "col", axis=1, tiled=True)
        arrived = [whole[:, i * block : (i + 1) * block] for i in range(8)]

    pieces = [own_piece] + arrived if direct else arrived
    spectra = jax.ShapeDtypeStruct((2 * column_vars, share), jnp.bfloat16)
    flat, *parts = pl.pallas_call(
        functools.partial(main_kernel, blocks, block, index_of),
        out_shape=[jax.ShapeDtypeStruct((blocks * column_vars, block), jnp.bfloat16)]
        + [spectra] * (bands - 1),
        in_specs=[VMEM_SPEC] * (5 + blocks),
        out_specs=[VMEM_SPEC] * bands,
        scratch_shapes=[pltpu.VMEM((blocks * column_vars, block), jnp.float32)],
        compiler_params=pltpu.CompilerParams(vmem_limit_bytes=24 * 1024 * 1024),
        cost_estimate=pl.CostEstimate(
            flops=4 * column_vars * width * (waves_total - share),
            bytes_accessed=4 * column_vars * width,
            transcendentals=0,
        ),
        name="column_and_waves",
    )(coriolis, mix, far_table, phase, kept, *pieces)
    ready = []
    for step, part in zip(held, parts):
        pairs = [(i, partner(i, step, bands)) for i in range(bands)]
        ready.append(lax.ppermute(part, "band", pairs))
    ready.append(
        pl.pallas_call(
            own_kernel,
            out_shape=spectra,
            in_specs=[VMEM_SPEC] * 3,
            out_specs=VMEM_SPEC,
            compiler_params=pltpu.CompilerParams(vmem_limit_bytes=24 * 1024 * 1024),
            cost_estimate=pl.CostEstimate(
                flops=4 * column_vars * width * share,
                bytes_accessed=4 * column_vars * width,
                transcendentals=0,
            ),
            name="own_waves",
        )(flat, own_table, phase)
    )
    return pl.pallas_call(
        functools.partial(place_kernel, held),
        out_shape=jax.ShapeDtypeStruct((1, 2, column_vars, bands, share), jnp.bfloat16),
        in_specs=[VMEM_SPEC] * bands,
        out_specs=VMEM_SPEC,
        compiler_params=pltpu.CompilerParams(vmem_limit_bytes=16 * 1024 * 1024),
        name="row_slots",
    )(*ready)


def solution(mesh):
    return jax.shard_map(
        functools.partial(body, mesh.shape["col"], mesh.shape["band"]),
        mesh=mesh,
        in_specs=(
            P("col", None, "band", None),
            P(None, "band", "col"),
            P(),
            P("band"),
            P("band"),
            P(),
        ),
        out_specs=P("col", None, None, None, "band"),
        check_vma=False,
    )
```

```python
import functools
import math

import jax
import jax.numpy as jnp
from jax import lax
from jax.experimental import pallas as pl
from jax.experimental.pallas import tpu as pltpu
from jax.sharding import PartitionSpec as P

LEVELS = 8
LATITUDES = 2560
LANES = 128
SUB = 32


def partner(place, step, count):
    if count & (count - 1) == 0:
        return place ^ step
    return (place + step) % count


def source(place, step, count):
    if count & (count - 1) == 0:
        return place ^ step
    return (place - step) % count


def turn(places, waves, points):
    product = places * waves
    whole = jnp.floor(product * (1.0 / points) + 0.5)
    quarter = (product - whole * points) * 4.0 / points
    nearest = jnp.floor(quarter + 0.5)
    angle = (quarter - nearest) * (0.5 * math.pi)
    square = angle * angle
    sine = angle + angle * square * (
        -1.6666654611e-1 + square * (8.3321608736e-3 - square * 1.9515295891e-4)
    )
    cosine = (
        1.0
        - 0.5 * square
        + square
        * square
        * (4.166664568298827e-2 + square * (-1.388731625493765e-3 + square * 2.443315711809948e-5))
    )
    odd = jnp.abs(nearest) == 1.0
    first = jnp.where(odd, sine, cosine)
    second = jnp.where(odd, cosine, sine)
    first = jnp.where((nearest == 1.0) | (jnp.abs(nearest) >= 2.0), -first, first)
    second = jnp.where((nearest == -1.0) | (jnp.abs(nearest) >= 2.0), -second, second)
    return first, -second


def tables_kernel(
    blocks, block, held, index_of, lat_ref, waves_hbm, coupling_hbm, tend_hbm, traj_hbm, *refs
):
    far_table_ref, own_table_ref, phase_ref, mix_ref, kept_ref, own_ref, coriolis_ref = refs[:7]
    waves_ref, coupling_ref, tend_ref, sems = refs[7:]
    copies = [
        pltpu.make_async_copy(source_ref, target_ref, sems.at[i])
        for i, (source_ref, target_ref) in enumerate(
            [
                (waves_hbm, waves_ref),
                (coupling_hbm, coupling_ref),
                (tend_hbm, tend_ref),
                (traj_hbm, own_ref),
            ]
        )
    ]
    for copy in copies:
        copy.start()
    index = lat_ref[0]
    count = jnp.minimum(20 + 4 * jnp.minimum(index, LATITUDES - 1 - index), tend_ref.shape[1])
    copies[0].wait()
    waves_total = waves_ref.shape[0]
    points = jnp.full((1, 1), count, jnp.int32).astype(jnp.float32)
    waves = waves_ref[...].reshape(1, waves_total).astype(jnp.float32)
    bands = len(held)
    share = waves_total // bands
    shares = [waves[:, d * share : (d + 1) * share] for d in range(bands)]
    my_band = lax.axis_index("band")
    ordered = []
    for step in held:
        goal = partner(my_band, step, bands)
        chosen = shares[0]
        for d in range(1, bands):
            chosen = jnp.where(goal == d, shares[d], chosen)
        ordered.append(chosen)
    waves = jnp.concatenate(ordered, axis=1)

    coarse_rows = block // SUB
    coarse_pad = -(-coarse_rows // 8) * 8
    fine = lax.broadcasted_iota(jnp.int32, (SUB, 1), 0).astype(jnp.float32)
    coarse = lax.broadcasted_iota(jnp.int32, (coarse_pad, 1), 0).astype(jnp.float32) * SUB
    fine_cos, fine_sin = turn(fine, waves, points)
    coarse_cos, coarse_sin = turn(coarse, waves, points)
    for row in range(coarse_rows):
        here_cos = coarse_cos[row : row + 1]
        here_sin = coarse_sin[row : row + 1]
        rows = pl.ds(row * SUB, SUB)
        table_cos = (here_cos * fine_cos - here_sin * fine_sin).astype(jnp.bfloat16)
        table_sin = (here_cos * fine_sin + here_sin * fine_cos).astype(jnp.bfloat16)
        far = far_table_ref.shape[1] // 2
        near = own_table_ref.shape[1] // 2
        far_table_ref[rows, :far] = table_cos[:, :far]
        far_table_ref[rows, far:] = table_sin[:, :far]
        own_table_ref[rows, :near] = table_cos[:, waves_total - near :]
        own_table_ref[rows, near:] = table_sin[:, waves_total - near :]

    slot = lax.broadcasted_iota(jnp.int32, (blocks, 1), 0)
    first = jnp.zeros((blocks, 1), jnp.int32)
    for i, of_row in enumerate(index_of()):
        first = jnp.where(slot == i, of_row * block, first)
    phase_cos, phase_sin = turn(first.astype(jnp.float32), waves, points)
    scale = jnp.where(2.0 * waves < points, 1.0 / jnp.sqrt(points), 0.0)
    phase_ref[0] = phase_cos * scale
    phase_ref[1] = phase_sin * scale

    latitude = jnp.full((1, LANES), index, jnp.int32).astype(jnp.float32)
    ratio = (2.0 * latitude + 1.0) / LATITUDES
    coriolis_ref[...] = turn(0.25 * (ratio - 1.0), jnp.ones((1, LANES), jnp.float32), 1.0)[1]

    copies[1].wait()
    column_vars = coupling_ref.shape[0]
    coupling = coupling_ref[...]
    row = lax.broadcasted_iota(jnp.int32, (column_vars, 3 * column_vars), 0)
    col = lax.broadcasted_iota(jnp.int32, (column_vars, 3 * column_vars), 1)
    near = (col == row).astype(jnp.bfloat16)
    far = ((col == row + column_vars) | (col == row + 2 * column_vars)).astype(jnp.bfloat16)
    mix_ref[...] = jnp.concatenate(
        [
            jnp.dot(coupling, near, preferred_element_type=jnp.float32),
            lax.dot_general(
                coupling, far, (((0,), (0,)), ((), ())), preferred_element_type=jnp.float32
            ),
        ],
        axis=0,
    ).astype(jnp.bfloat16)

    copies[2].wait()
    for i in range(blocks):
        cols = slice(i * block, (i + 1) * block)
        place = i * block + lax.broadcasted_iota(jnp.int32, (1, block), 1)
        kept_ref[:, cols] = jnp.where(
            place < count, tend_ref[:, cols].astype(jnp.float32), 0.0
        ).astype(jnp.bfloat16)
    copies[3].wait()


def transform(flat, column_vars, table_ref, phase_ref, first_wave):
    wide = table_ref.shape[1]
    waves = wide // 2
    near = jnp.concatenate(
        [
            jnp.dot(flat, table_ref[:, i : min(i + 256, wide)], preferred_element_type=jnp.float32)
            for i in range(0, wide, 256)
        ],
        axis=1,
    )
    real = jnp.zeros((column_vars, waves), jnp.float32)
    imag = jnp.zeros((column_vars, waves), jnp.float32)
    for i in range(flat.shape[0] // column_vars):
        rows = slice(i * column_vars, (i + 1) * column_vars)
        near_cos, near_sin = near[rows, :waves], near[rows, waves:]
        far_cos = phase_ref[0, i : i + 1, first_wave : first_wave + waves]
        far_sin = phase_ref[1, i : i + 1, first_wave : first_wave + waves]
        real = real + (far_cos * near_cos - far_sin * near_sin)
        imag = imag + (far_cos * near_sin + far_sin * near_cos)
    return jnp.concatenate([real, imag], axis=0)


def main_kernel(blocks, block, index_of, *refs):
    coriolis_ref, mix_ref, table_ref, phase_ref, tend_ref = refs[:5]
    traj_refs = refs[5 : 5 + blocks]
    flat_ref = refs[5 + blocks]
    out_refs = refs[6 + blocks : -1]
    grid_ref = refs[-1]
    column_vars = tend_ref.shape[0]
    coriolis = coriolis_ref[:, :1]
    mix = mix_ref[...]
    for i, index in enumerate(index_of()):
        start = pl.multiple_of(index * block, LANES)
        traj = traj_refs[i][...].astype(jnp.float32)
        tend = tend_ref[:, pl.ds(start, block)].astype(jnp.float32)
        stacked = jnp.concatenate([traj, tend, tend * traj], axis=0).astype(jnp.bfloat16)
        mixed = jnp.dot(mix, stacked, preferred_element_type=jnp.float32)
        total = mixed[column_vars:] + tend * mixed[:column_vars]
        grid_ref[pl.ds(i * column_vars, column_vars), :] = jnp.concatenate(
            [
                total[:LEVELS] - coriolis * tend[LEVELS : 2 * LEVELS],
                total[LEVELS : 2 * LEVELS] + coriolis * tend[:LEVELS],
                total[2 * LEVELS :],
            ],
            axis=0,
        )
    flat = grid_ref[...].astype(jnp.bfloat16)
    flat_ref[...] = flat
    both = transform(flat, column_vars, table_ref, phase_ref, 0)
    share = out_refs[0].shape[1]
    for k, out_ref in enumerate(out_refs):
        out_ref[...] = both[:, k * share : (k + 1) * share].astype(jnp.bfloat16)


def own_kernel(flat_ref, table_ref, phase_ref, out_ref):
    near = table_ref.shape[1] // 2
    column_vars, share = out_ref.shape[0] // 2, out_ref.shape[1]
    both = transform(
        flat_ref[...], column_vars, table_ref, phase_ref, phase_ref.shape[2] - near
    )
    out_ref[...] = both[:, near - share :].astype(jnp.bfloat16)


def place_kernel(held, *refs):
    parts = len(held)
    in_refs = refs[:parts]
    out_ref = refs[parts]
    column_vars = out_ref.shape[2]
    share = out_ref.shape[4]
    total = parts * column_vars
    row = lax.broadcasted_iota(jnp.int32, (total, 1), 0)
    variable = jnp.floor((row.astype(jnp.float32) + 0.5) * (1.0 / parts)).astype(jnp.int32)
    slot = row - variable * parts
    if parts & (parts - 1) == 0:
        step = slot ^ lax.axis_index("band")
    else:
        step = lax.axis_index("band") - slot
        step = jnp.where(step < 0, step + parts, step)
    target = variable
    for position, which in enumerate(held):
        target = jnp.where(step == which, target + position * column_vars, target)
    choose = (target == lax.broadcasted_iota(jnp.int32, (total, total), 1)).astype(jnp.bfloat16)
    wide = [ref[...].astype(jnp.float32) for ref in in_refs]
    for half in range(2):
        rows = slice(half * column_vars, (half + 1) * column_vars)
        stacked = jnp.concatenate([w[rows] for w in wide], axis=0).astype(jnp.bfloat16)
        placed = jnp.dot(choose, stacked, preferred_element_type=jnp.float32)
        out_ref[0, half] = placed.reshape(column_vars, parts, share).astype(jnp.bfloat16)


VMEM_SPEC = pl.BlockSpec(memory_space=pltpu.VMEM)
SMEM_SPEC = pl.BlockSpec(memory_space=pltpu.SMEM)
HBM_SPEC = pl.BlockSpec(memory_space=pltpu.HBM)


def body(cols, bands, adjoint_tend, trajectory, coupling, row_lat, row_points, wave_order):
    column_vars = adjoint_tend.shape[1]
    width = adjoint_tend.shape[3]
    own = trajectory.shape[2]
    waves_total = wave_order.shape[0]
    share = waves_total // bands
    tend = adjoint_tend.reshape(column_vars, width)
    traj = trajectory.reshape(column_vars, own)

    direct = own % LANES == 0 and cols > 1 and cols & (cols - 1) == 0
    across = cols // 2
    swaps = [2, 3, 5, 4, 7, 1, 6] if cols == 8 else list(range(1, cols))
    far = -(-(waves_total - share) // LANES) * LANES
    near = waves_total - (waves_total - share) // LANES * LANES
    blocks = cols if direct else 8
    held = list(reversed(range(bands)))
    block = width // blocks

    def index_of():
        if not direct:
            return list(range(blocks))
        my_col = lax.axis_index("col")
        return [my_col] + [my_col ^ swap for swap in swaps]

    operands = [wave_order, coupling, tend, traj]
    far_table, own_table, phase, mix, kept, own_piece, coriolis = pl.pallas_call(
        functools.partial(tables_kernel, blocks, block, held, index_of),
        out_shape=[
            jax.ShapeDtypeStruct((block, 2 * far), jnp.bfloat16),
            jax.ShapeDtypeStruct((block, 2 * near), jnp.bfloat16),
            jax.ShapeDtypeStruct((2, blocks, waves_total), jnp.float32),
            jax.ShapeDtypeStruct((2 * column_vars, 3 * column_vars), jnp.bfloat16),
            jax.ShapeDtypeStruct((column_vars, width), jnp.bfloat16),
            jax.ShapeDtypeStruct((column_vars, own), jnp.bfloat16),
            jax.ShapeDtypeStruct((1, LANES), jnp.float32),
        ],
        in_specs=[SMEM_SPEC] + [HBM_SPEC] * len(operands),
        out_specs=[VMEM_SPEC] * 7,
        scratch_shapes=[
            pltpu.VMEM((waves_total,), jnp.int32),
            pltpu.VMEM((column_vars, column_vars), jnp.bfloat16),
            pltpu.VMEM((column_vars, width), jnp.bfloat16),
            pltpu.SemaphoreType.DMA((len(operands),)),
        ],
        compiler_params=pltpu.CompilerParams(vmem_limit_bytes=16 * 1024 * 1024),
        cost_estimate=pl.CostEstimate(
            flops=1024 * column_vars * width, bytes_accessed=4 * column_vars * width, transcendentals=0
        ),
        name="tables",
    )(row_lat, *[pltpu.with_memory_space_constraint(x, pltpu.HBM) for x in operands])

    if direct:
        swapped = lambda x, swap: lax.ppermute(x, "col", [(i, i ^ swap) for i in range(cols)])
        moved = {across: swapped(traj, across)}
        for swap in swaps:
            if across < swap < cols - 1:
                moved[swap] = swapped(moved[across], swap ^ across)
            elif swap != across:
                moved[swap] = swapped(traj, swap)
        arrived = [moved[swap] for swap in swaps]
    else:
        whole = lax.all_gather(traj, "col", axis=1, tiled=True)
        arrived = [whole[:, i * block : (i + 1) * block] for i in range(8)]

    pieces = [own_piece] + arrived if direct else arrived
    spectra = jax.ShapeDtypeStruct((2 * column_vars, share), jnp.bfloat16)
    flat, *parts = pl.pallas_call(
        functools.partial(main_kernel, blocks, block, index_of),
        out_shape=[jax.ShapeDtypeStruct((blocks * column_vars, block), jnp.bfloat16)]
        + [spectra] * (bands - 1),
        in_specs=[VMEM_SPEC] * (5 + blocks),
        out_specs=[VMEM_SPEC] * bands,
        scratch_shapes=[pltpu.VMEM((blocks * column_vars, block), jnp.float32)],
        compiler_params=pltpu.CompilerParams(vmem_limit_bytes=24 * 1024 * 1024),
        cost_estimate=pl.CostEstimate(
            flops=4 * column_vars * width * (waves_total - share),
            bytes_accessed=4 * column_vars * width,
            transcendentals=0,
        ),
        name="column_and_waves",
    )(coriolis, mix, far_table, phase, kept, *pieces)
    ready = []
    for step, part in zip(held, parts):
        pairs = [(i, partner(i, step, bands)) for i in range(bands)]
        ready.append(lax.ppermute(part, "band", pairs))
    ready.append(
        pl.pallas_call(
            own_kernel,
            out_shape=spectra,
            in_specs=[VMEM_SPEC] * 3,
            out_specs=VMEM_SPEC,
            compiler_params=pltpu.CompilerParams(vmem_limit_bytes=24 * 1024 * 1024),
            cost_estimate=pl.CostEstimate(
                flops=4 * column_vars * width * share,
                bytes_accessed=4 * column_vars * width,
                transcendentals=0,
            ),
            name="own_waves",
        )(flat, own_table, phase)
    )
    return pl.pallas_call(
        functools.partial(place_kernel, held),
        out_shape=jax.ShapeDtypeStruct((1, 2, column_vars, bands, share), jnp.bfloat16),
        in_specs=[VMEM_SPEC] * bands,
        out_specs=VMEM_SPEC,
        compiler_params=pltpu.CompilerParams(vmem_limit_bytes=16 * 1024 * 1024),
        name="row_slots",
    )(*ready)


def solution(mesh):
    return jax.shard_map(
        functools.partial(body, mesh.shape["col"], mesh.shape["band"]),
        mesh=mesh,
        in_specs=(
            P("col", None, "band", None),
            P(None, "band", "col"),
            P(),
            P("band"),
            P("band"),
            P(),
        ),
        out_specs=P("col", None, None, None, "band"),
        check_vma=False,
    )
```

```python
import functools
import math

import jax
import jax.numpy as jnp
from jax import lax
from jax.experimental import pallas as pl
from jax.experimental.pallas import tpu as pltpu
from jax.sharding import PartitionSpec as P

LEVELS = 8
LATITUDES = 2560
LANES = 128
SUB = 32


def partner(place, step, count):
    if count & (count - 1) == 0:
        return place ^ step
    return (place + step) % count


def source(place, step, count):
    if count & (count - 1) == 0:
        return place ^ step
    return (place - step) % count


def turn(places, waves, points):
    product = places * waves
    whole = jnp.floor(product * (1.0 / points) + 0.5)
    quarter = (product - whole * points) * 4.0 / points
    nearest = jnp.floor(quarter + 0.5)
    angle = (quarter - nearest) * (0.5 * math.pi)
    square = angle * angle
    sine = angle + angle * square * (
        -1.6666654611e-1 + square * (8.3321608736e-3 - square * 1.9515295891e-4)
    )
    cosine = (
        1.0
        - 0.5 * square
        + square
        * square
        * (4.166664568298827e-2 + square * (-1.388731625493765e-3 + square * 2.443315711809948e-5))
    )
    odd = jnp.abs(nearest) == 1.0
    first = jnp.where(odd, sine, cosine)
    second = jnp.where(odd, cosine, sine)
    first = jnp.where((nearest == 1.0) | (jnp.abs(nearest) >= 2.0), -first, first)
    second = jnp.where((nearest == -1.0) | (jnp.abs(nearest) >= 2.0), -second, second)
    return first, -second


def column_step(block, indices, mix, coriolis, tend_ref, traj_refs, grid_ref):
    column_vars = tend_ref.shape[0]
    for i, (index, traj_ref) in enumerate(zip(indices, traj_refs)):
        start = pl.multiple_of(index * block, LANES)
        traj = traj_ref[...].astype(jnp.float32)
        tend = tend_ref[:, pl.ds(start, block)].astype(jnp.float32)
        stacked = jnp.concatenate([traj, tend, tend * traj], axis=0).astype(jnp.bfloat16)
        mixed = jnp.dot(mix, stacked, preferred_element_type=jnp.float32)
        total = mixed[column_vars:] + tend * mixed[:column_vars]
        grid_ref[pl.ds(i * column_vars, column_vars), :] = jnp.concatenate(
            [
                total[:LEVELS] - coriolis * tend[LEVELS : 2 * LEVELS],
                total[LEVELS : 2 * LEVELS] + coriolis * tend[:LEVELS],
                total[2 * LEVELS :],
            ],
            axis=0,
        )


def tables_kernel(
    blocks, block, early, held, index_of, lat_ref, waves_hbm, coupling_hbm, tend_hbm, traj_hbm, *refs
):
    early_refs, refs = refs[: max(early - 1, 0)], refs[max(early - 1, 0) :]
    far_table_ref, own_table_ref, phase_ref, mix_ref, kept_ref, coriolis_ref = refs[:6]
    waves_ref, coupling_ref, tend_ref, own_ref, sems = refs[6 + (early > 0) :]
    copies = [
        pltpu.make_async_copy(source_ref, target_ref, sems.at[i])
        for i, (source_ref, target_ref) in enumerate(
            [
                (waves_hbm, waves_ref),
                (coupling_hbm, coupling_ref),
                (tend_hbm, tend_ref),
                (traj_hbm, own_ref),
            ]
        )
    ]
    for copy in copies:
        copy.start()
    index = lat_ref[0]
    count = jnp.minimum(20 + 4 * jnp.minimum(index, LATITUDES - 1 - index), tend_ref.shape[1])
    copies[0].wait()
    waves_total = waves_ref.shape[0]
    points = jnp.full((1, 1), count, jnp.int32).astype(jnp.float32)
    waves = waves_ref[...].reshape(1, waves_total).astype(jnp.float32)
    bands = len(held)
    share = waves_total // bands
    shares = [waves[:, d * share : (d + 1) * share] for d in range(bands)]
    my_band = lax.axis_index("band")
    ordered = []
    for step in held:
        goal = partner(my_band, step, bands)
        chosen = shares[0]
        for d in range(1, bands):
            chosen = jnp.where(goal == d, shares[d], chosen)
        ordered.append(chosen)
    waves = jnp.concatenate(ordered, axis=1)

    coarse_rows = block // SUB
    coarse_pad = -(-coarse_rows // 8) * 8
    fine = lax.broadcasted_iota(jnp.int32, (SUB, 1), 0).astype(jnp.float32)
    coarse = lax.broadcasted_iota(jnp.int32, (coarse_pad, 1), 0).astype(jnp.float32) * SUB
    fine_cos, fine_sin = turn(fine, waves, points)
    coarse_cos, coarse_sin = turn(coarse, waves, points)
    for row in range(coarse_rows):
        here_cos = coarse_cos[row : row + 1]
        here_sin = coarse_sin[row : row + 1]
        rows = pl.ds(row * SUB, SUB)
        table_cos = (here_cos * fine_cos - here_sin * fine_sin).astype(jnp.bfloat16)
        table_sin = (here_cos * fine_sin + here_sin * fine_cos).astype(jnp.bfloat16)
        far = far_table_ref.shape[1] // 2
        near = own_table_ref.shape[1] // 2
        far_table_ref[rows, :far] = table_cos[:, :far]
        far_table_ref[rows, far:] = table_sin[:, :far]
        own_table_ref[rows, :near] = table_cos[:, waves_total - near :]
        own_table_ref[rows, near:] = table_sin[:, waves_total - near :]

    slot = lax.broadcasted_iota(jnp.int32, (blocks, 1), 0)
    first = jnp.zeros((blocks, 1), jnp.int32)
    for i, of_row in enumerate(index_of()):
        first = jnp.where(slot == i, of_row * block, first)
    phase_cos, phase_sin = turn(first.astype(jnp.float32), waves, points)
    scale = jnp.where(2.0 * waves < points, 1.0 / jnp.sqrt(points), 0.0)
    phase_ref[0] = phase_cos * scale
    phase_ref[1] = phase_sin * scale

    latitude = jnp.full((1, LANES), index, jnp.int32).astype(jnp.float32)
    ratio = (2.0 * latitude + 1.0) / LATITUDES
    coriolis_ref[...] = turn(0.25 * (ratio - 1.0), jnp.ones((1, LANES), jnp.float32), 1.0)[1]

    copies[1].wait()
    column_vars = coupling_ref.shape[0]
    coupling = coupling_ref[...]
    row = lax.broadcasted_iota(jnp.int32, (column_vars, 3 * column_vars), 0)
    col = lax.broadcasted_iota(jnp.int32, (column_vars, 3 * column_vars), 1)
    near = (col == row).astype(jnp.bfloat16)
    far = ((col == row + column_vars) | (col == row + 2 * column_vars)).astype(jnp.bfloat16)
    mix_ref[...] = jnp.concatenate(
        [
            jnp.dot(coupling, near, preferred_element_type=jnp.float32),
            lax.dot_general(
                coupling, far, (((0,), (0,)), ((), ())), preferred_element_type=jnp.float32
            ),
        ],
        axis=0,
    ).astype(jnp.bfloat16)

    copies[2].wait()
    for i in range(blocks):
        cols = slice(i * block, (i + 1) * block)
        place = i * block + lax.broadcasted_iota(jnp.int32, (1, block), 1)
        kept_ref[:, cols] = jnp.where(
            place < count, tend_ref[:, cols].astype(jnp.float32), 0.0
        ).astype(jnp.bfloat16)
    copies[3].wait()
    if early:
        column_step(
            block,
            index_of()[:early],
            mix_ref[...],
            coriolis_ref[:, :1],
            kept_ref,
            [own_ref, *early_refs],
            refs[6],
        )


def transform(flat, column_vars, table_ref, phase_ref, first_wave):
    wide = table_ref.shape[1]
    waves = wide // 2
    near = jnp.concatenate(
        [
            jnp.dot(flat, table_ref[:, i : min(i + 256, wide)], preferred_element_type=jnp.float32)
            for i in range(0, wide, 256)
        ],
        axis=1,
    )
    real = jnp.zeros((column_vars, waves), jnp.float32)
    imag = jnp.zeros((column_vars, waves), jnp.float32)
    for i in range(flat.shape[0] // column_vars):
        rows = slice(i * column_vars, (i + 1) * column_vars)
        near_cos, near_sin = near[rows, :waves], near[rows, waves:]
        far_cos = phase_ref[0, i : i + 1, first_wave : first_wave + waves]
        far_sin = phase_ref[1, i : i + 1, first_wave : first_wave + waves]
        real = real + (far_cos * near_cos - far_sin * near_sin)
        imag = imag + (far_cos * near_sin + far_sin * near_cos)
    return jnp.concatenate([real, imag], axis=0)


def main_kernel(blocks, block, early, index_of, *refs):
    coriolis_ref, mix_ref, table_ref, phase_ref, tend_ref = refs[:5]
    before, refs = refs[5 : 5 + (early > 0)], refs[5 + (early > 0) :]
    late = blocks - early
    flat_ref = refs[late]
    out_refs = refs[late + 1 : -1]
    column_vars = tend_ref.shape[0]
    column_step(
        block,
        index_of()[early:],
        mix_ref[...],
        coriolis_ref[:, :1],
        tend_ref,
        refs[:late],
        refs[-1],
    )
    flat = jnp.concatenate([ref[...] for ref in before] + [refs[-1][...]], axis=0)
    flat = flat.astype(jnp.bfloat16)
    flat_ref[...] = flat
    both = transform(flat, column_vars, table_ref, phase_ref, 0)
    share = out_refs[0].shape[1]
    for k, out_ref in enumerate(out_refs):
        out_ref[...] = both[:, k * share : (k + 1) * share].astype(jnp.bfloat16)


def own_kernel(flat_ref, table_ref, phase_ref, out_ref):
    near = table_ref.shape[1] // 2
    column_vars, share = out_ref.shape[0] // 2, out_ref.shape[1]
    both = transform(
        flat_ref[...], column_vars, table_ref, phase_ref, phase_ref.shape[2] - near
    )
    out_ref[...] = both[:, near - share :].astype(jnp.bfloat16)


def place_kernel(held, *refs):
    parts = len(held)
    in_refs = refs[:parts]
    out_ref = refs[parts]
    column_vars = out_ref.shape[2]
    share = out_ref.shape[4]
    total = parts * column_vars
    row = lax.broadcasted_iota(jnp.int32, (total, 1), 0)
    variable = jnp.floor((row.astype(jnp.float32) + 0.5) * (1.0 / parts)).astype(jnp.int32)
    slot = row - variable * parts
    if parts & (parts - 1) == 0:
        step = slot ^ lax.axis_index("band")
    else:
        step = lax.axis_index("band") - slot
        step = jnp.where(step < 0, step + parts, step)
    target = variable
    for position, which in enumerate(held):
        target = jnp.where(step == which, target + position * column_vars, target)
    choose = (target == lax.broadcasted_iota(jnp.int32, (total, total), 1)).astype(jnp.bfloat16)
    wide = [ref[...].astype(jnp.float32) for ref in in_refs]
    for half in range(2):
        rows = slice(half * column_vars, (half + 1) * column_vars)
        stacked = jnp.concatenate([w[rows] for w in wide], axis=0).astype(jnp.bfloat16)
        placed = jnp.dot(choose, stacked, preferred_element_type=jnp.float32)
        out_ref[0, half] = placed.reshape(column_vars, parts, share).astype(jnp.bfloat16)


VMEM_SPEC = pl.BlockSpec(memory_space=pltpu.VMEM)
SMEM_SPEC = pl.BlockSpec(memory_space=pltpu.SMEM)
HBM_SPEC = pl.BlockSpec(memory_space=pltpu.HBM)


def body(cols, bands, adjoint_tend, trajectory, coupling, row_lat, row_points, wave_order):
    column_vars = adjoint_tend.shape[1]
    width = adjoint_tend.shape[3]
    own = trajectory.shape[2]
    waves_total = wave_order.shape[0]
    share = waves_total // bands
    tend = adjoint_tend.reshape(column_vars, width)
    traj = trajectory.reshape(column_vars, own)

    direct = own % LANES == 0 and cols > 1 and cols & (cols - 1) == 0
    across = cols // 2
    swaps = [1, across]
    late_swaps = [2, 3, 5, 7, 6] if cols == 8 else [q for q in range(2, cols) if q != across]
    far = -(-(waves_total - share) // LANES) * LANES
    near = waves_total - (waves_total - share) // LANES * LANES
    blocks = cols if direct else 8
    held = list(reversed(range(bands)))
    block = width // blocks

    def index_of():
        if not direct:
            return list(range(blocks))
        my_col = lax.axis_index("col")
        return [my_col] + [my_col ^ swap for swap in [*swaps, *late_swaps]]

    if direct:
        swapped = lambda x, swap: lax.ppermute(x, "col", [(i, i ^ swap) for i in range(cols)])
        moved = {across: swapped(traj, across)}
        for swap in swaps:
            if swap != across:
                moved[swap] = swapped(traj, swap)
        first = [moved[swap] for swap in swaps]
        pieces = [
            swapped(moved[across], swap ^ across)
            if across < swap < cols - 1
            else swapped(traj, swap)
            for swap in late_swaps
        ]
        early = 1 + len(first)
    else:
        whole = lax.all_gather(traj, "col", axis=1, tiled=True)
        first = []
        pieces = [whole[:, i * block : (i + 1) * block] for i in range(8)]
        early = 0

    operands = [wave_order, coupling, tend, traj]
    far_table, own_table, phase, mix, kept, coriolis, *before = pl.pallas_call(
        functools.partial(tables_kernel, blocks, block, early, held, index_of),
        out_shape=[
            jax.ShapeDtypeStruct((block, 2 * far), jnp.bfloat16),
            jax.ShapeDtypeStruct((block, 2 * near), jnp.bfloat16),
            jax.ShapeDtypeStruct((2, blocks, waves_total), jnp.float32),
            jax.ShapeDtypeStruct((2 * column_vars, 3 * column_vars), jnp.bfloat16),
            jax.ShapeDtypeStruct((column_vars, width), jnp.bfloat16),
            jax.ShapeDtypeStruct((1, LANES), jnp.float32),
        ]
        + [jax.ShapeDtypeStruct((early * column_vars, block), jnp.float32)] * (early > 0),
        in_specs=[SMEM_SPEC] + [HBM_SPEC] * len(operands) + [VMEM_SPEC] * len(first),
        out_specs=[VMEM_SPEC] * (6 + (early > 0)),
        scratch_shapes=[
            pltpu.VMEM((waves_total,), jnp.int32),
            pltpu.VMEM((column_vars, column_vars), jnp.bfloat16),
            pltpu.VMEM((column_vars, width), jnp.bfloat16),
            pltpu.VMEM((column_vars, own), jnp.bfloat16),
            pltpu.SemaphoreType.DMA((len(operands),)),
        ],
        compiler_params=pltpu.CompilerParams(vmem_limit_bytes=16 * 1024 * 1024),
        cost_estimate=pl.CostEstimate(
            flops=1024 * column_vars * width, bytes_accessed=4 * column_vars * width, transcendentals=0
        ),
        name="tables",
    )(row_lat, *[pltpu.with_memory_space_constraint(x, pltpu.HBM) for x in operands], *first)

    spectra = jax.ShapeDtypeStruct((2 * column_vars, share), jnp.bfloat16)
    flat, *parts = pl.pallas_call(
        functools.partial(main_kernel, blocks, block, early, index_of),
        out_shape=[jax.ShapeDtypeStruct((blocks * column_vars, block), jnp.bfloat16)]
        + [spectra] * (bands - 1),
        in_specs=[VMEM_SPEC] * (5 + len(before) + len(pieces)),
        out_specs=[VMEM_SPEC] * bands,
        scratch_shapes=[pltpu.VMEM(((blocks - early) * column_vars, block), jnp.float32)],
        compiler_params=pltpu.CompilerParams(vmem_limit_bytes=24 * 1024 * 1024),
        cost_estimate=pl.CostEstimate(
            flops=4 * column_vars * width * (waves_total - share),
            bytes_accessed=4 * column_vars * width,
            transcendentals=0,
        ),
        name="column_and_waves",
    )(coriolis, mix, far_table, phase, kept, *before, *pieces)
    ready = []
    for step, part in zip(held, parts):
        pairs = [(i, partner(i, step, bands)) for i in range(bands)]
        ready.append(lax.ppermute(part, "band", pairs))
    ready.append(
        pl.pallas_call(
            own_kernel,
            out_shape=spectra,
            in_specs=[VMEM_SPEC] * 3,
            out_specs=VMEM_SPEC,
            compiler_params=pltpu.CompilerParams(vmem_limit_bytes=24 * 1024 * 1024),
            cost_estimate=pl.CostEstimate(
                flops=4 * column_vars * width * share,
                bytes_accessed=4 * column_vars * width,
                transcendentals=0,
            ),
            name="own_waves",
        )(flat, own_table, phase)
    )
    return pl.pallas_call(
        functools.partial(place_kernel, held),
        out_shape=jax.ShapeDtypeStruct((1, 2, column_vars, bands, share), jnp.bfloat16),
        in_specs=[VMEM_SPEC] * bands,
        out_specs=VMEM_SPEC,
        compiler_params=pltpu.CompilerParams(vmem_limit_bytes=16 * 1024 * 1024),
        name="row_slots",
    )(*ready)


def solution(mesh):
    return jax.shard_map(
        functools.partial(body, mesh.shape["col"], mesh.shape["band"]),
        mesh=mesh,
        in_specs=(
            P("col", None, "band", None),
            P(None, "band", "col"),
            P(),
            P("band"),
            P("band"),
            P(),
        ),
        out_specs=P("col", None, None, None, "band"),
        check_vma=False,
    )
```

```python
import functools
import math

import jax
import jax.numpy as jnp
from jax import lax
from jax.experimental import pallas as pl
from jax.experimental.pallas import tpu as pltpu
from jax.sharding import PartitionSpec as P

LEVELS = 8
LATITUDES = 2560
LANES = 128
SUB = 32


def partner(place, step, count):
    if count & (count - 1) == 0:
        return place ^ step
    return (place + step) % count


def source(place, step, count):
    if count & (count - 1) == 0:
        return place ^ step
    return (place - step) % count


def turn(places, waves, points):
    product = places * waves
    whole = jnp.floor(product * (1.0 / points) + 0.5)
    quarter = (product - whole * points) * 4.0 / points
    nearest = jnp.floor(quarter + 0.5)
    angle = (quarter - nearest) * (0.5 * math.pi)
    square = angle * angle
    sine = angle + angle * square * (
        -1.6666654611e-1 + square * (8.3321608736e-3 - square * 1.9515295891e-4)
    )
    cosine = (
        1.0
        - 0.5 * square
        + square
        * square
        * (4.166664568298827e-2 + square * (-1.388731625493765e-3 + square * 2.443315711809948e-5))
    )
    odd = jnp.abs(nearest) == 1.0
    first = jnp.where(odd, sine, cosine)
    second = jnp.where(odd, cosine, sine)
    first = jnp.where((nearest == 1.0) | (jnp.abs(nearest) >= 2.0), -first, first)
    second = jnp.where((nearest == -1.0) | (jnp.abs(nearest) >= 2.0), -second, second)
    return first, -second


def column_step(block, indices, mix, coriolis, tend_ref, traj_refs, grid_ref):
    column_vars = tend_ref.shape[0]
    for i, (index, traj_ref) in enumerate(zip(indices, traj_refs)):
        start = pl.multiple_of(index * block, LANES)
        traj = traj_ref[...].astype(jnp.float32)
        tend = tend_ref[:, pl.ds(start, block)].astype(jnp.float32)
        stacked = jnp.concatenate([traj, tend, tend * traj], axis=0).astype(jnp.bfloat16)
        mixed = jnp.dot(mix, stacked, preferred_element_type=jnp.float32)
        total = mixed[column_vars:] + tend * mixed[:column_vars]
        grid_ref[pl.ds(i * column_vars, column_vars), :] = jnp.concatenate(
            [
                total[:LEVELS] - coriolis * tend[LEVELS : 2 * LEVELS],
                total[LEVELS : 2 * LEVELS] + coriolis * tend[:LEVELS],
                total[2 * LEVELS :],
            ],
            axis=0,
        )


def tables_kernel(
    blocks, block, early, held, index_of, lat_ref, waves_hbm, coupling_hbm, tend_hbm, traj_hbm, *refs
):
    early_refs, refs = refs[: max(early - 1, 0)], refs[max(early - 1, 0) :]
    far_table_ref, own_table_ref, phase_ref, mix_ref, kept_ref, coriolis_ref = refs[:6]
    waves_ref, coupling_ref, tend_ref, own_ref, sems = refs[6 + (early > 0) :]
    copies = [
        pltpu.make_async_copy(source_ref, target_ref, sems.at[i])
        for i, (source_ref, target_ref) in enumerate(
            [
                (waves_hbm, waves_ref),
                (coupling_hbm, coupling_ref),
                (tend_hbm, tend_ref),
                (traj_hbm, own_ref),
            ]
        )
    ]
    for copy in copies:
        copy.start()
    index = lat_ref[0]
    count = jnp.minimum(20 + 4 * jnp.minimum(index, LATITUDES - 1 - index), tend_ref.shape[1])
    copies[0].wait()
    waves_total = waves_ref.shape[0]
    points = jnp.full((1, 1), count, jnp.int32).astype(jnp.float32)
    waves = waves_ref[...].reshape(1, waves_total).astype(jnp.float32)
    bands = len(held)
    share = waves_total // bands
    shares = [waves[:, d * share : (d + 1) * share] for d in range(bands)]
    my_band = lax.axis_index("band")
    ordered = []
    for step in held:
        goal = partner(my_band, step, bands)
        chosen = shares[0]
        for d in range(1, bands):
            chosen = jnp.where(goal == d, shares[d], chosen)
        ordered.append(chosen)
    waves = jnp.concatenate(ordered, axis=1)

    coarse_rows = block // SUB
    coarse_pad = -(-coarse_rows // 8) * 8
    fine = lax.broadcasted_iota(jnp.int32, (SUB, 1), 0).astype(jnp.float32)
    coarse = lax.broadcasted_iota(jnp.int32, (coarse_pad, 1), 0).astype(jnp.float32) * SUB
    fine_cos, fine_sin = turn(fine, waves, points)
    coarse_cos, coarse_sin = turn(coarse, waves, points)
    for row in range(coarse_rows):
        here_cos = coarse_cos[row : row + 1]
        here_sin = coarse_sin[row : row + 1]
        rows = pl.ds(row * SUB, SUB)
        table_cos = (here_cos * fine_cos - here_sin * fine_sin).astype(jnp.bfloat16)
        table_sin = (here_cos * fine_sin + here_sin * fine_cos).astype(jnp.bfloat16)
        far = far_table_ref.shape[1] // 2
        near = own_table_ref.shape[1] // 2
        far_table_ref[rows, :far] = table_cos[:, :far]
        far_table_ref[rows, far:] = table_sin[:, :far]
        own_table_ref[rows, :near] = table_cos[:, waves_total - near :]
        own_table_ref[rows, near:] = table_sin[:, waves_total - near :]

    slot = lax.broadcasted_iota(jnp.int32, (blocks, 1), 0)
    first = jnp.zeros((blocks, 1), jnp.int32)
    for i, of_row in enumerate(index_of()):
        first = jnp.where(slot == i, of_row * block, first)
    phase_cos, phase_sin = turn(first.astype(jnp.float32), waves, points)
    scale = jnp.where(2.0 * waves < points, 1.0 / jnp.sqrt(points), 0.0)
    phase_ref[0] = phase_cos * scale
    phase_ref[1] = phase_sin * scale

    latitude = jnp.full((1, LANES), index, jnp.int32).astype(jnp.float32)
    ratio = (2.0 * latitude + 1.0) / LATITUDES
    coriolis_ref[...] = turn(0.25 * (ratio - 1.0), jnp.ones((1, LANES), jnp.float32), 1.0)[1]

    copies[1].wait()
    column_vars = coupling_ref.shape[0]
    coupling = coupling_ref[...]
    row = lax.broadcasted_iota(jnp.int32, (column_vars, 3 * column_vars), 0)
    col = lax.broadcasted_iota(jnp.int32, (column_vars, 3 * column_vars), 1)
    near = (col == row).astype(jnp.bfloat16)
    far = ((col == row + column_vars) | (col == row + 2 * column_vars)).astype(jnp.bfloat16)
    mix_ref[...] = jnp.concatenate(
        [
            jnp.dot(coupling, near, preferred_element_type=jnp.float32),
            lax.dot_general(
                coupling, far, (((0,), (0,)), ((), ())), preferred_element_type=jnp.float32
            ),
        ],
        axis=0,
    ).astype(jnp.bfloat16)

    copies[2].wait()
    for i in range(blocks):
        cols = slice(i * block, (i + 1) * block)
        place = i * block + lax.broadcasted_iota(jnp.int32, (1, block), 1)
        kept_ref[:, cols] = jnp.where(
            place < count, tend_ref[:, cols].astype(jnp.float32), 0.0
        ).astype(jnp.bfloat16)
    copies[3].wait()
    if early:
        column_step(
            block,
            index_of()[:early],
            mix_ref[...],
            coriolis_ref[:, :1],
            kept_ref,
            [own_ref, *early_refs],
            refs[6],
        )


def transform(flat, column_vars, table_ref, phase_ref, first_wave):
    wide = table_ref.shape[1]
    waves = wide // 2
    near = jnp.concatenate(
        [
            jnp.dot(flat, table_ref[:, i : min(i + 256, wide)], preferred_element_type=jnp.float32)
            for i in range(0, wide, 256)
        ],
        axis=1,
    )
    real = jnp.zeros((column_vars, waves), jnp.float32)
    imag = jnp.zeros((column_vars, waves), jnp.float32)
    for i in range(flat.shape[0] // column_vars):
        rows = slice(i * column_vars, (i + 1) * column_vars)
        near_cos, near_sin = near[rows, :waves], near[rows, waves:]
        far_cos = phase_ref[0, i : i + 1, first_wave : first_wave + waves]
        far_sin = phase_ref[1, i : i + 1, first_wave : first_wave + waves]
        real = real + (far_cos * near_cos - far_sin * near_sin)
        imag = imag + (far_cos * near_sin + far_sin * near_cos)
    return jnp.concatenate([real, imag], axis=0)


def main_kernel(blocks, block, early, index_of, *refs):
    coriolis_ref, mix_ref, table_ref, phase_ref, tend_ref = refs[:5]
    before, refs = refs[5 : 5 + (early > 0)], refs[5 + (early > 0) :]
    late = blocks - early
    flat_ref = refs[late]
    out_refs = refs[late + 1 : -1]
    column_vars = tend_ref.shape[0]
    column_step(
        block,
        index_of()[early:],
        mix_ref[...],
        coriolis_ref[:, :1],
        tend_ref,
        refs[:late],
        refs[-1],
    )
    flat = jnp.concatenate([ref[...] for ref in before] + [refs[-1][...]], axis=0)
    flat = flat.astype(jnp.bfloat16)
    flat_ref[...] = flat
    both = transform(flat, column_vars, table_ref, phase_ref, 0)
    share = out_refs[0].shape[1]
    for k, out_ref in enumerate(out_refs):
        out_ref[...] = both[:, k * share : (k + 1) * share].astype(jnp.bfloat16)


def own_kernel(held, flat_ref, table_ref, phase_ref, out_ref, choose_ref):
    near = table_ref.shape[1] // 2
    column_vars, share = out_ref.shape[0] // 2, out_ref.shape[1]
    both = transform(
        flat_ref[...], column_vars, table_ref, phase_ref, phase_ref.shape[2] - near
    )
    out_ref[...] = both[:, near - share :].astype(jnp.bfloat16)

    parts = len(held)
    total = choose_ref.shape[0]
    row = lax.broadcasted_iota(jnp.int32, (total, 1), 0)
    variable = jnp.floor((row.astype(jnp.float32) + 0.5) * (1.0 / parts)).astype(jnp.int32)
    slot = row - variable * parts
    if parts & (parts - 1) == 0:
        step = slot ^ lax.axis_index("band")
    else:
        step = lax.axis_index("band") - slot
        step = jnp.where(step < 0, step + parts, step)
    target = variable
    for position, which in enumerate(held):
        target = jnp.where(step == which, target + position * column_vars, target)
    choose_ref[...] = (target == lax.broadcasted_iota(jnp.int32, (total, total), 1)).astype(
        jnp.bfloat16
    )


def place_kernel(choose_ref, *refs):
    in_refs, out_ref = refs[:-1], refs[-1]
    _, _, column_vars, parts, share = out_ref.shape
    choose = choose_ref[...]
    wide = [ref[...].astype(jnp.float32) for ref in in_refs]
    for half in range(2):
        rows = slice(half * column_vars, (half + 1) * column_vars)
        stacked = jnp.concatenate([w[rows] for w in wide], axis=0).astype(jnp.bfloat16)
        placed = jnp.dot(choose, stacked, preferred_element_type=jnp.float32)
        out_ref[0, half] = placed.reshape(column_vars, parts, share).astype(jnp.bfloat16)


VMEM_SPEC = pl.BlockSpec(memory_space=pltpu.VMEM)
SMEM_SPEC = pl.BlockSpec(memory_space=pltpu.SMEM)
HBM_SPEC = pl.BlockSpec(memory_space=pltpu.HBM)


def body(cols, bands, adjoint_tend, trajectory, coupling, row_lat, row_points, wave_order):
    column_vars = adjoint_tend.shape[1]
    width = adjoint_tend.shape[3]
    own = trajectory.shape[2]
    waves_total = wave_order.shape[0]
    share = waves_total // bands
    tend = adjoint_tend.reshape(column_vars, width)
    traj = trajectory.reshape(column_vars, own)

    direct = own % LANES == 0 and cols > 2 and cols & (cols - 1) == 0
    across = cols // 2
    swaps = [1, across]
    late_swaps = [2, 3, 5, 7, 6] if cols == 8 else [q for q in range(2, cols) if q != across]
    far = -(-(waves_total - share) // LANES) * LANES
    near = waves_total - (waves_total - share) // LANES * LANES
    blocks = cols if direct else 8
    held = list(reversed(range(bands)))
    block = width // blocks

    def index_of():
        if not direct:
            return list(range(blocks))
        my_col = lax.axis_index("col")
        return [my_col] + [my_col ^ swap for swap in [*swaps, *late_swaps]]

    if direct:
        swapped = lambda x, swap: lax.ppermute(x, "col", [(i, i ^ swap) for i in range(cols)])
        moved = {across: swapped(traj, across)}
        for swap in swaps:
            if swap != across:
                moved[swap] = swapped(traj, swap)
        first = [moved[swap] for swap in swaps]
        pieces = [
            swapped(moved[across], swap ^ across)
            if across < swap < cols - 1
            else swapped(traj, swap)
            for swap in late_swaps
        ]
        early = 1 + len(first)
    else:
        whole = lax.all_gather(traj, "col", axis=1, tiled=True)
        first = []
        pieces = [whole[:, i * block : (i + 1) * block] for i in range(8)]
        early = 0

    operands = [wave_order, coupling, tend, traj]
    far_table, own_table, phase, mix, kept, coriolis, *before = pl.pallas_call(
        functools.partial(tables_kernel, blocks, block, early, held, index_of),
        out_shape=[
            jax.ShapeDtypeStruct((block, 2 * far), jnp.bfloat16),
            jax.ShapeDtypeStruct((block, 2 * near), jnp.bfloat16),
            jax.ShapeDtypeStruct((2, blocks, waves_total), jnp.float32),
            jax.ShapeDtypeStruct((2 * column_vars, 3 * column_vars), jnp.bfloat16),
            jax.ShapeDtypeStruct((column_vars, width), jnp.bfloat16),
            jax.ShapeDtypeStruct((1, LANES), jnp.float32),
        ]
        + [jax.ShapeDtypeStruct((early * column_vars, block), jnp.float32)] * (early > 0),
        in_specs=[SMEM_SPEC] + [HBM_SPEC] * len(operands) + [VMEM_SPEC] * len(first),
        out_specs=[VMEM_SPEC] * (6 + (early > 0)),
        scratch_shapes=[
            pltpu.VMEM((waves_total,), jnp.int32),
            pltpu.VMEM((column_vars, column_vars), jnp.bfloat16),
            pltpu.VMEM((column_vars, width), jnp.bfloat16),
            pltpu.VMEM((column_vars, own), jnp.bfloat16),
            pltpu.SemaphoreType.DMA((len(operands),)),
        ],
        compiler_params=pltpu.CompilerParams(vmem_limit_bytes=16 * 1024 * 1024),
        cost_estimate=pl.CostEstimate(
            flops=1024 * column_vars * width, bytes_accessed=4 * column_vars * width, transcendentals=0
        ),
        name="tables",
    )(row_lat, *[pltpu.with_memory_space_constraint(x, pltpu.HBM) for x in operands], *first)

    spectra = jax.ShapeDtypeStruct((2 * column_vars, share), jnp.bfloat16)
    flat, *parts = pl.pallas_call(
        functools.partial(main_kernel, blocks, block, early, index_of),
        out_shape=[jax.ShapeDtypeStruct((blocks * column_vars, block), jnp.bfloat16)]
        + [spectra] * (bands - 1),
        in_specs=[VMEM_SPEC] * (5 + len(before) + len(pieces)),
        out_specs=[VMEM_SPEC] * bands,
        scratch_shapes=[pltpu.VMEM(((blocks - early) * column_vars, block), jnp.float32)],
        compiler_params=pltpu.CompilerParams(vmem_limit_bytes=24 * 1024 * 1024),
        cost_estimate=pl.CostEstimate(
            flops=4 * column_vars * width * (waves_total - share),
            bytes_accessed=4 * column_vars * width,
            transcendentals=0,
        ),
        name="column_and_waves",
    )(coriolis, mix, far_table, phase, kept, *before, *pieces)
    ready = []
    for step, part in zip(held, parts):
        pairs = [(i, partner(i, step, bands)) for i in range(bands)]
        ready.append(lax.ppermute(part, "band", pairs))
    total = bands * column_vars
    own_part, choose = pl.pallas_call(
        functools.partial(own_kernel, held),
        out_shape=[spectra, jax.ShapeDtypeStruct((total, total), jnp.bfloat16)],
        in_specs=[VMEM_SPEC] * 3,
        out_specs=[VMEM_SPEC] * 2,
        compiler_params=pltpu.CompilerParams(vmem_limit_bytes=24 * 1024 * 1024),
        cost_estimate=pl.CostEstimate(
            flops=4 * column_vars * width * share,
            bytes_accessed=4 * column_vars * width,
            transcendentals=0,
        ),
        name="own_waves",
    )(flat, own_table, phase)
    return pl.pallas_call(
        place_kernel,
        out_shape=jax.ShapeDtypeStruct((1, 2, column_vars, bands, share), jnp.bfloat16),
        in_specs=[VMEM_SPEC] * (1 + bands),
        out_specs=VMEM_SPEC,
        compiler_params=pltpu.CompilerParams(vmem_limit_bytes=16 * 1024 * 1024),
        name="row_slots",
    )(choose, *ready, own_part)


def solution(mesh):
    return jax.shard_map(
        functools.partial(body, mesh.shape["col"], mesh.shape["band"]),
        mesh=mesh,
        in_specs=(
            P("col", None, "band", None),
            P(None, "band", "col"),
            P(),
            P("band"),
            P("band"),
            P(),
        ),
        out_specs=P("col", None, None, None, "band"),
        check_vma=False,
    )
```

```python
import functools
import math

import jax
import jax.numpy as jnp
from jax import lax
from jax.experimental import pallas as pl
from jax.experimental.pallas import tpu as pltpu
from jax.sharding import PartitionSpec as P

LEVELS = 8
LATITUDES = 2560
LANES = 128
SUB = 32


def partner(place, step, count):
    if count & (count - 1) == 0:
        return place ^ step
    return (place + step) % count


def source(place, step, count):
    if count & (count - 1) == 0:
        return place ^ step
    return (place - step) % count


def turn(places, waves, points):
    product = places * waves
    whole = jnp.floor(product * (1.0 / points) + 0.5)
    quarter = (product - whole * points) * 4.0 / points
    nearest = jnp.floor(quarter + 0.5)
    angle = (quarter - nearest) * (0.5 * math.pi)
    square = angle * angle
    sine = angle + angle * square * (
        -1.6666654611e-1 + square * (8.3321608736e-3 - square * 1.9515295891e-4)
    )
    cosine = (
        1.0
        - 0.5 * square
        + square
        * square
        * (4.166664568298827e-2 + square * (-1.388731625493765e-3 + square * 2.443315711809948e-5))
    )
    odd = jnp.abs(nearest) == 1.0
    first = jnp.where(odd, sine, cosine)
    second = jnp.where(odd, cosine, sine)
    first = jnp.where((nearest == 1.0) | (jnp.abs(nearest) >= 2.0), -first, first)
    second = jnp.where((nearest == -1.0) | (jnp.abs(nearest) >= 2.0), -second, second)
    return first, -second


def column_step(block, indices, mix, coriolis, tend_ref, traj_refs, grid_ref):
    column_vars = tend_ref.shape[0]
    for i, (index, traj_ref) in enumerate(zip(indices, traj_refs)):
        start = pl.multiple_of(index * block, LANES)
        traj = traj_ref[...].astype(jnp.float32)
        tend = tend_ref[:, pl.ds(start, block)].astype(jnp.float32)
        stacked = jnp.concatenate([traj, tend, tend * traj], axis=0).astype(jnp.bfloat16)
        mixed = jnp.dot(mix, stacked, preferred_element_type=jnp.float32)
        total = mixed[column_vars:] + tend * mixed[:column_vars]
        grid_ref[pl.ds(i * column_vars, column_vars), :] = jnp.concatenate(
            [
                total[:LEVELS] - coriolis * tend[LEVELS : 2 * LEVELS],
                total[LEVELS : 2 * LEVELS] + coriolis * tend[:LEVELS],
                total[2 * LEVELS :],
            ],
            axis=0,
        )


def tables_kernel(
    blocks, block, early, held, index_of, lat_ref, waves_hbm, coupling_hbm, tend_hbm, traj_hbm, *refs
):
    early_refs, refs = refs[: max(early - 1, 0)], refs[max(early - 1, 0) :]
    far_table_ref, own_table_ref, phase_ref, mix_ref, kept_ref, coriolis_ref = refs[:6]
    waves_ref, coupling_ref, tend_ref, own_ref, sems = refs[6 + (early > 0) :]
    copies = [
        pltpu.make_async_copy(source_ref, target_ref, sems.at[i])
        for i, (source_ref, target_ref) in enumerate(
            [
                (waves_hbm, waves_ref),
                (coupling_hbm, coupling_ref),
                (tend_hbm, tend_ref),
                (traj_hbm, own_ref),
            ]
        )
    ]
    for copy in copies:
        copy.start()
    index = lat_ref[0]
    count = jnp.minimum(20 + 4 * jnp.minimum(index, LATITUDES - 1 - index), tend_ref.shape[1])
    copies[0].wait()
    waves_total = waves_ref.shape[0]
    points = jnp.full((1, 1), count, jnp.int32).astype(jnp.float32)
    waves = waves_ref[...].reshape(1, waves_total).astype(jnp.float32)
    bands = len(held)
    share = waves_total // bands
    shares = [waves[:, d * share : (d + 1) * share] for d in range(bands)]
    my_band = lax.axis_index("band")
    ordered = []
    for step in held:
        goal = partner(my_band, step, bands)
        chosen = shares[0]
        for d in range(1, bands):
            chosen = jnp.where(goal == d, shares[d], chosen)
        ordered.append(chosen)
    waves = jnp.concatenate(ordered, axis=1)

    coarse_rows = block // SUB
    coarse_pad = -(-coarse_rows // 8) * 8
    fine = lax.broadcasted_iota(jnp.int32, (SUB, 1), 0).astype(jnp.float32)
    coarse = lax.broadcasted_iota(jnp.int32, (coarse_pad, 1), 0).astype(jnp.float32) * SUB
    fine_cos, fine_sin = turn(fine, waves, points)
    coarse_cos, coarse_sin = turn(coarse, waves, points)
    for row in range(coarse_rows):
        here_cos = coarse_cos[row : row + 1]
        here_sin = coarse_sin[row : row + 1]
        rows = pl.ds(row * SUB, SUB)
        table_cos = (here_cos * fine_cos - here_sin * fine_sin).astype(jnp.bfloat16)
        table_sin = (here_cos * fine_sin + here_sin * fine_cos).astype(jnp.bfloat16)
        for ref, skip in [
            (far_table_ref, 0),
            (own_table_ref, waves_total - own_table_ref.shape[1] // 2),
        ]:
            for i in range(0, ref.shape[1] // 2, LANES):
                cols = slice(skip + i, skip + i + LANES)
                ref[rows, 2 * i : 2 * i + LANES] = table_cos[:, cols]
                ref[rows, 2 * i + LANES : 2 * (i + LANES)] = table_sin[:, cols]

    slot = lax.broadcasted_iota(jnp.int32, (blocks, 1), 0)
    first = jnp.zeros((blocks, 1), jnp.int32)
    for i, of_row in enumerate(index_of()):
        first = jnp.where(slot == i, of_row * block, first)
    phase_cos, phase_sin = turn(first.astype(jnp.float32), waves, points)
    scale = jnp.where(2.0 * waves < points, 1.0 / jnp.sqrt(points), 0.0)
    phase_ref[0] = phase_cos * scale
    phase_ref[1] = phase_sin * scale

    latitude = jnp.full((1, LANES), index, jnp.int32).astype(jnp.float32)
    ratio = (2.0 * latitude + 1.0) / LATITUDES
    coriolis_ref[...] = turn(0.25 * (ratio - 1.0), jnp.ones((1, LANES), jnp.float32), 1.0)[1]

    copies[1].wait()
    column_vars = coupling_ref.shape[0]
    coupling = coupling_ref[...]
    row = lax.broadcasted_iota(jnp.int32, (column_vars, 3 * column_vars), 0)
    col = lax.broadcasted_iota(jnp.int32, (column_vars, 3 * column_vars), 1)
    near = (col == row).astype(jnp.bfloat16)
    far = ((col == row + column_vars) | (col == row + 2 * column_vars)).astype(jnp.bfloat16)
    mix_ref[...] = jnp.concatenate(
        [
            jnp.dot(coupling, near, preferred_element_type=jnp.float32),
            lax.dot_general(
                coupling, far, (((0,), (0,)), ((), ())), preferred_element_type=jnp.float32
            ),
        ],
        axis=0,
    ).astype(jnp.bfloat16)

    copies[2].wait()
    for i in range(blocks):
        cols = slice(i * block, (i + 1) * block)
        place = i * block + lax.broadcasted_iota(jnp.int32, (1, block), 1)
        kept_ref[:, cols] = jnp.where(
            place < count, tend_ref[:, cols].astype(jnp.float32), 0.0
        ).astype(jnp.bfloat16)
    copies[3].wait()
    if early:
        column_step(
            block,
            index_of()[:early],
            mix_ref[...],
            coriolis_ref[:, :1],
            kept_ref,
            [own_ref, *early_refs],
            refs[6],
        )


def transform(flat, column_vars, table_ref, phase_ref, first_wave):
    reals, imags = [], []
    for i in range(0, table_ref.shape[1] // 2, LANES):
        near = jnp.dot(
            flat, table_ref[:, 2 * i : 2 * (i + LANES)], preferred_element_type=jnp.float32
        )
        cols = slice(first_wave + i, first_wave + i + LANES)
        real = jnp.zeros((column_vars, LANES), jnp.float32)
        imag = jnp.zeros((column_vars, LANES), jnp.float32)
        for k in range(flat.shape[0] // column_vars):
            rows = slice(k * column_vars, (k + 1) * column_vars)
            near_cos, near_sin = near[rows, :LANES], near[rows, LANES:]
            far_cos, far_sin = phase_ref[0, k : k + 1, cols], phase_ref[1, k : k + 1, cols]
            real = real + (far_cos * near_cos - far_sin * near_sin)
            imag = imag + (far_cos * near_sin + far_sin * near_cos)
        reals.append(real)
        imags.append(imag)
    return jnp.concatenate(
        [jnp.concatenate(reals, axis=1), jnp.concatenate(imags, axis=1)], axis=0
    )


def main_kernel(blocks, block, early, index_of, *refs):
    coriolis_ref, mix_ref, table_ref, phase_ref, tend_ref = refs[:5]
    before, refs = refs[5 : 5 + (early > 0)], refs[5 + (early > 0) :]
    late = blocks - early
    flat_ref = refs[late]
    out_refs = refs[late + 1 : -1]
    column_vars = tend_ref.shape[0]
    column_step(
        block,
        index_of()[early:],
        mix_ref[...],
        coriolis_ref[:, :1],
        tend_ref,
        refs[:late],
        refs[-1],
    )
    flat = jnp.concatenate([ref[...] for ref in before] + [refs[-1][...]], axis=0)
    flat = flat.astype(jnp.bfloat16)
    flat_ref[...] = flat
    both = transform(flat, column_vars, table_ref, phase_ref, 0)
    share = out_refs[0].shape[1]
    for k, out_ref in enumerate(out_refs):
        out_ref[...] = both[:, k * share : (k + 1) * share].astype(jnp.bfloat16)


def own_kernel(flat_ref, table_ref, phase_ref, out_ref):
    near = table_ref.shape[1] // 2
    column_vars, share = out_ref.shape[0] // 2, out_ref.shape[1]
    both = transform(
        flat_ref[...], column_vars, table_ref, phase_ref, phase_ref.shape[2] - near
    )
    out_ref[...] = both[:, near - share :].astype(jnp.bfloat16)


def place_kernel(held, *refs):
    parts = len(held)
    in_refs = refs[:parts]
    out_ref = refs[parts]
    column_vars = out_ref.shape[2]
    share = out_ref.shape[4]
    total = parts * column_vars
    row = lax.broadcasted_iota(jnp.int32, (total, 1), 0)
    variable = jnp.floor((row.astype(jnp.float32) + 0.5) * (1.0 / parts)).astype(jnp.int32)
    slot = row - variable * parts
    if parts & (parts - 1) == 0:
        step = slot ^ lax.axis_index("band")
    else:
        step = lax.axis_index("band") - slot
        step = jnp.where(step < 0, step + parts, step)
    target = variable
    for position, which in enumerate(held):
        target = jnp.where(step == which, target + position * column_vars, target)
    choose = (target == lax.broadcasted_iota(jnp.int32, (total, total), 1)).astype(jnp.bfloat16)
    wide = [ref[...].astype(jnp.float32) for ref in in_refs]
    for half in range(2):
        rows = slice(half * column_vars, (half + 1) * column_vars)
        stacked = jnp.concatenate([w[rows] for w in wide], axis=0).astype(jnp.bfloat16)
        placed = jnp.dot(choose, stacked, preferred_element_type=jnp.float32)
        out_ref[0, half] = placed.reshape(column_vars, parts, share).astype(jnp.bfloat16)


VMEM_SPEC = pl.BlockSpec(memory_space=pltpu.VMEM)
SMEM_SPEC = pl.BlockSpec(memory_space=pltpu.SMEM)
HBM_SPEC = pl.BlockSpec(memory_space=pltpu.HBM)


def body(cols, bands, adjoint_tend, trajectory, coupling, row_lat, row_points, wave_order):
    column_vars = adjoint_tend.shape[1]
    width = adjoint_tend.shape[3]
    own = trajectory.shape[2]
    waves_total = wave_order.shape[0]
    share = waves_total // bands
    tend = adjoint_tend.reshape(column_vars, width)
    traj = trajectory.reshape(column_vars, own)

    direct = own % LANES == 0 and cols > 1 and cols & (cols - 1) == 0
    across = cols // 2
    swaps = [1, across]
    late_swaps = [2, 3, 5, 7, 6] if cols == 8 else [q for q in range(2, cols) if q != across]
    far = -(-(waves_total - share) // LANES) * LANES
    near = waves_total - (waves_total - share) // LANES * LANES
    blocks = cols if direct else 8
    held = list(reversed(range(bands)))
    block = width // blocks

    def index_of():
        if not direct:
            return list(range(blocks))
        my_col = lax.axis_index("col")
        return [my_col] + [my_col ^ swap for swap in [*swaps, *late_swaps]]

    if direct:
        swapped = lambda x, swap: lax.ppermute(x, "col", [(i, i ^ swap) for i in range(cols)])
        moved = {across: swapped(traj, across)}
        for swap in swaps:
            if swap != across:
                moved[swap] = swapped(traj, swap)
        first = [moved[swap] for swap in swaps]
        pieces = [
            swapped(moved[across], swap ^ across)
            if across < swap < cols - 1
            else swapped(traj, swap)
            for swap in late_swaps
        ]
        early = 1 + len(first)
    else:
        whole = lax.all_gather(traj, "col", axis=1, tiled=True)
        first = []
        pieces = [whole[:, i * block : (i + 1) * block] for i in range(8)]
        early = 0

    operands = [wave_order, coupling, tend, traj]
    far_table, own_table, phase, mix, kept, coriolis, *before = pl.pallas_call(
        functools.partial(tables_kernel, blocks, block, early, held, index_of),
        out_shape=[
            jax.ShapeDtypeStruct((block, 2 * far), jnp.bfloat16),
            jax.ShapeDtypeStruct((block, 2 * near), jnp.bfloat16),
            jax.ShapeDtypeStruct((2, blocks, waves_total), jnp.float32),
            jax.ShapeDtypeStruct((2 * column_vars, 3 * column_vars), jnp.bfloat16),
            jax.ShapeDtypeStruct((column_vars, width), jnp.bfloat16),
            jax.ShapeDtypeStruct((1, LANES), jnp.float32),
        ]
        + [jax.ShapeDtypeStruct((early * column_vars, block), jnp.float32)] * (early > 0),
        in_specs=[SMEM_SPEC] + [HBM_SPEC] * len(operands) + [VMEM_SPEC] * len(first),
        out_specs=[VMEM_SPEC] * (6 + (early > 0)),
        scratch_shapes=[
            pltpu.VMEM((waves_total,), jnp.int32),
            pltpu.VMEM((column_vars, column_vars), jnp.bfloat16),
            pltpu.VMEM((column_vars, width), jnp.bfloat16),
            pltpu.VMEM((column_vars, own), jnp.bfloat16),
            pltpu.SemaphoreType.DMA((len(operands),)),
        ],
        compiler_params=pltpu.CompilerParams(vmem_limit_bytes=16 * 1024 * 1024),
        cost_estimate=pl.CostEstimate(
            flops=1024 * column_vars * width, bytes_accessed=4 * column_vars * width, transcendentals=0
        ),
        name="tables",
    )(row_lat, *[pltpu.with_memory_space_constraint(x, pltpu.HBM) for x in operands], *first)

    spectra = jax.ShapeDtypeStruct((2 * column_vars, share), jnp.bfloat16)
    flat, *parts = pl.pallas_call(
        functools.partial(main_kernel, blocks, block, early, index_of),
        out_shape=[jax.ShapeDtypeStruct((blocks * column_vars, block), jnp.bfloat16)]
        + [spectra] * (bands - 1),
        in_specs=[VMEM_SPEC] * (5 + len(before) + len(pieces)),
        out_specs=[VMEM_SPEC] * bands,
        scratch_shapes=[pltpu.VMEM(((blocks - early) * column_vars, block), jnp.float32)],
        compiler_params=pltpu.CompilerParams(vmem_limit_bytes=24 * 1024 * 1024),
        cost_estimate=pl.CostEstimate(
            flops=4 * column_vars * width * (waves_total - share),
            bytes_accessed=4 * column_vars * width,
            transcendentals=0,
        ),
        name="column_and_waves",
    )(coriolis, mix, far_table, phase, kept, *before, *pieces)
    ready = []
    for step, part in zip(held, parts):
        pairs = [(i, partner(i, step, bands)) for i in range(bands)]
        ready.append(lax.ppermute(part, "band", pairs))
    ready.append(
        pl.pallas_call(
            own_kernel,
            out_shape=spectra,
            in_specs=[VMEM_SPEC] * 3,
            out_specs=VMEM_SPEC,
            compiler_params=pltpu.CompilerParams(vmem_limit_bytes=24 * 1024 * 1024),
            cost_estimate=pl.CostEstimate(
                flops=4 * column_vars * width * share,
                bytes_accessed=4 * column_vars * width,
                transcendentals=0,
            ),
            name="own_waves",
        )(flat, own_table, phase)
    )
    return pl.pallas_call(
        functools.partial(place_kernel, held),
        out_shape=jax.ShapeDtypeStruct((1, 2, column_vars, bands, share), jnp.bfloat16),
        in_specs=[VMEM_SPEC] * bands,
        out_specs=VMEM_SPEC,
        compiler_params=pltpu.CompilerParams(vmem_limit_bytes=16 * 1024 * 1024),
        name="row_slots",
    )(*ready)


def solution(mesh):
    return jax.shard_map(
        functools.partial(body, mesh.shape["col"], mesh.shape["band"]),
        mesh=mesh,
        in_specs=(
            P("col", None, "band", None),
            P(None, "band", "col"),
            P(),
            P("band"),
            P("band"),
            P(),
        ),
        out_specs=P("col", None, None, None, "band"),
        check_vma=False,
    )
```

```python
import functools
import math

import jax
import jax.numpy as jnp
from jax import lax
from jax.experimental import pallas as pl
from jax.experimental.pallas import tpu as pltpu
from jax.sharding import PartitionSpec as P

LEVELS = 8
LATITUDES = 2560
LANES = 128
SUB = 32


def partner(place, step, count):
    if count & (count - 1) == 0:
        return place ^ step
    return (place + step) % count


def source(place, step, count):
    if count & (count - 1) == 0:
        return place ^ step
    return (place - step) % count


def turn(places, waves, points):
    product = places * waves
    whole = jnp.floor(product * (1.0 / points) + 0.5)
    quarter = (product - whole * points) * 4.0 / points
    nearest = jnp.floor(quarter + 0.5)
    angle = (quarter - nearest) * (0.5 * math.pi)
    square = angle * angle
    sine = angle + angle * square * (
        -1.6666654611e-1 + square * (8.3321608736e-3 - square * 1.9515295891e-4)
    )
    cosine = (
        1.0
        - 0.5 * square
        + square
        * square
        * (4.166664568298827e-2 + square * (-1.388731625493765e-3 + square * 2.443315711809948e-5))
    )
    odd = jnp.abs(nearest) == 1.0
    first = jnp.where(odd, sine, cosine)
    second = jnp.where(odd, cosine, sine)
    first = jnp.where((nearest == 1.0) | (jnp.abs(nearest) >= 2.0), -first, first)
    second = jnp.where((nearest == -1.0) | (jnp.abs(nearest) >= 2.0), -second, second)
    return first, -second


def column_step(block, indices, mix, coriolis, tend_ref, traj_refs, grid_ref):
    column_vars = tend_ref.shape[0]
    for i, (index, traj_ref) in enumerate(zip(indices, traj_refs)):
        start = pl.multiple_of(index * block, LANES)
        traj = traj_ref[...].astype(jnp.float32)
        tend = tend_ref[:, pl.ds(start, block)].astype(jnp.float32)
        stacked = jnp.concatenate([traj, tend, tend * traj], axis=0).astype(jnp.bfloat16)
        mixed = jnp.dot(mix, stacked, preferred_element_type=jnp.float32)
        total = mixed[column_vars:] + tend * mixed[:column_vars]
        grid_ref[pl.ds(i * column_vars, column_vars), :] = jnp.concatenate(
            [
                total[:LEVELS] - coriolis * tend[LEVELS : 2 * LEVELS],
                total[LEVELS : 2 * LEVELS] + coriolis * tend[:LEVELS],
                total[2 * LEVELS :],
            ],
            axis=0,
        )


def tables_kernel(
    blocks, block, early, held, index_of, lat_ref, waves_hbm, coupling_hbm, tend_hbm, traj_hbm, *refs
):
    early_refs, refs = refs[: max(early - 1, 0)], refs[max(early - 1, 0) :]
    far_table_ref, own_table_ref, phase_ref, mix_ref, kept_ref, coriolis_ref = refs[:6]
    waves_ref, coupling_ref, tend_ref, own_ref, sems = refs[6 + (early > 0) :]
    copies = [
        pltpu.make_async_copy(source_ref, target_ref, sems.at[i])
        for i, (source_ref, target_ref) in enumerate(
            [
                (waves_hbm, waves_ref),
                (coupling_hbm, coupling_ref),
                (tend_hbm, tend_ref),
                (traj_hbm, own_ref),
            ]
        )
    ]
    for copy in copies:
        copy.start()
    index = lat_ref[0]
    count = jnp.minimum(20 + 4 * jnp.minimum(index, LATITUDES - 1 - index), tend_ref.shape[1])
    copies[0].wait()
    waves_total = waves_ref.shape[0]
    points = jnp.full((1, 1), count, jnp.int32).astype(jnp.float32)
    waves = waves_ref[...].reshape(1, waves_total).astype(jnp.float32)
    bands = len(held)
    share = waves_total // bands
    shares = [waves[:, d * share : (d + 1) * share] for d in range(bands)]
    my_band = lax.axis_index("band")
    ordered = []
    for step in held:
        goal = partner(my_band, step, bands)
        chosen = shares[0]
        for d in range(1, bands):
            chosen = jnp.where(goal == d, shares[d], chosen)
        ordered.append(chosen)
    waves = jnp.concatenate(ordered, axis=1)

    coarse_rows = block // SUB
    coarse_pad = -(-coarse_rows // 8) * 8
    fine = lax.broadcasted_iota(jnp.int32, (SUB, 1), 0).astype(jnp.float32)
    coarse = lax.broadcasted_iota(jnp.int32, (coarse_pad, 1), 0).astype(jnp.float32) * SUB
    fine_cos, fine_sin = turn(fine, waves, points)
    coarse_cos, coarse_sin = turn(coarse, waves, points)
    for row in range(coarse_rows):
        here_cos = coarse_cos[row : row + 1]
        here_sin = coarse_sin[row : row + 1]
        rows = pl.ds(row * SUB, SUB)
        table_cos = (here_cos * fine_cos - here_sin * fine_sin).astype(jnp.bfloat16)
        table_sin = (here_cos * fine_sin + here_sin * fine_cos).astype(jnp.bfloat16)
        for ref, skip in [
            (far_table_ref, 0),
            (own_table_ref, waves_total - own_table_ref.shape[1] // 2),
        ]:
            for i in range(0, ref.shape[1] // 2, LANES):
                cols = slice(skip + i, skip + i + LANES)
                ref[rows, 2 * i : 2 * i + LANES] = table_cos[:, cols]
                ref[rows, 2 * i + LANES : 2 * (i + LANES)] = table_sin[:, cols]

    slot = lax.broadcasted_iota(jnp.int32, (blocks, 1), 0)
    first = jnp.zeros((blocks, 1), jnp.int32)
    for i, of_row in enumerate(index_of()):
        first = jnp.where(slot == i, of_row * block, first)
    phase_cos, phase_sin = turn(first.astype(jnp.float32), waves, points)
    scale = jnp.where(2.0 * waves < points, 1.0 / jnp.sqrt(points), 0.0)
    phase_ref[0] = phase_cos * scale
    phase_ref[1] = phase_sin * scale

    latitude = jnp.full((1, LANES), index, jnp.int32).astype(jnp.float32)
    ratio = (2.0 * latitude + 1.0) / LATITUDES
    coriolis_ref[...] = turn(0.25 * (ratio - 1.0), jnp.ones((1, LANES), jnp.float32), 1.0)[1]

    copies[1].wait()
    column_vars = coupling_ref.shape[0]
    coupling = coupling_ref[...]
    row = lax.broadcasted_iota(jnp.int32, (column_vars, 3 * column_vars), 0)
    col = lax.broadcasted_iota(jnp.int32, (column_vars, 3 * column_vars), 1)
    near = (col == row).astype(jnp.bfloat16)
    far = ((col == row + column_vars) | (col == row + 2 * column_vars)).astype(jnp.bfloat16)
    mix_ref[...] = jnp.concatenate(
        [
            jnp.dot(coupling, near, preferred_element_type=jnp.float32),
            lax.dot_general(
                coupling, far, (((0,), (0,)), ((), ())), preferred_element_type=jnp.float32
            ),
        ],
        axis=0,
    ).astype(jnp.bfloat16)

    copies[2].wait()
    for i in range(blocks):
        cols = slice(i * block, (i + 1) * block)
        place = i * block + lax.broadcasted_iota(jnp.int32, (1, block), 1)
        kept_ref[:, cols] = jnp.where(
            place < count, tend_ref[:, cols].astype(jnp.float32), 0.0
        ).astype(jnp.bfloat16)
    copies[3].wait()
    if early:
        column_step(
            block,
            index_of()[:early],
            mix_ref[...],
            coriolis_ref[:, :1],
            kept_ref,
            [own_ref, *early_refs],
            refs[6],
        )


def transform(flat, column_vars, table_ref, phase_ref, first_wave):
    reals, imags = [], []
    for i in range(0, table_ref.shape[1] // 2, LANES):
        near = jnp.dot(
            flat, table_ref[:, 2 * i : 2 * (i + LANES)], preferred_element_type=jnp.float32
        )
        cols = slice(first_wave + i, first_wave + i + LANES)
        real = jnp.zeros((column_vars, LANES), jnp.float32)
        imag = jnp.zeros((column_vars, LANES), jnp.float32)
        for k in range(flat.shape[0] // column_vars):
            rows = slice(k * column_vars, (k + 1) * column_vars)
            near_cos, near_sin = near[rows, :LANES], near[rows, LANES:]
            far_cos, far_sin = phase_ref[0, k : k + 1, cols], phase_ref[1, k : k + 1, cols]
            real = real + (far_cos * near_cos - far_sin * near_sin)
            imag = imag + (far_cos * near_sin + far_sin * near_cos)
        reals.append(real)
        imags.append(imag)
    return jnp.concatenate(
        [jnp.concatenate(reals, axis=1), jnp.concatenate(imags, axis=1)], axis=0
    )


def main_kernel(blocks, block, early, index_of, *refs):
    coriolis_ref, mix_ref, table_ref, phase_ref, tend_ref = refs[:5]
    before, refs = refs[5 : 5 + (early > 0)], refs[5 + (early > 0) :]
    late = blocks - early
    flat_ref = refs[late]
    out_refs = refs[late + 1 : -1]
    column_vars = tend_ref.shape[0]
    column_step(
        block,
        index_of()[early:],
        mix_ref[...],
        coriolis_ref[:, :1],
        tend_ref,
        refs[:late],
        refs[-1],
    )
    flat = jnp.concatenate([ref[...] for ref in before] + [refs[-1][...]], axis=0)
    flat = flat.astype(jnp.bfloat16)
    flat_ref[...] = flat
    both = transform(flat, column_vars, table_ref, phase_ref, 0)
    share = out_refs[0].shape[1]
    for k, out_ref in enumerate(out_refs):
        out_ref[...] = both[:, k * share : (k + 1) * share].astype(jnp.bfloat16)


def own_kernel(held, flat_ref, table_ref, phase_ref, out_ref, choose_ref):
    near = table_ref.shape[1] // 2
    column_vars, share = out_ref.shape[0] // 2, out_ref.shape[1]
    both = transform(
        flat_ref[...], column_vars, table_ref, phase_ref, phase_ref.shape[2] - near
    )
    out_ref[...] = both[:, near - share :].astype(jnp.bfloat16)

    parts = len(held)
    total = choose_ref.shape[0]
    row = lax.broadcasted_iota(jnp.int32, (total, 1), 0)
    variable = jnp.floor((row.astype(jnp.float32) + 0.5) * (1.0 / parts)).astype(jnp.int32)
    slot = row - variable * parts
    if parts & (parts - 1) == 0:
        step = slot ^ lax.axis_index("band")
    else:
        step = lax.axis_index("band") - slot
        step = jnp.where(step < 0, step + parts, step)
    target = variable
    for position, which in enumerate(held):
        target = jnp.where(step == which, target + position * column_vars, target)
    choose_ref[...] = (target == lax.broadcasted_iota(jnp.int32, (total, total), 1)).astype(
        jnp.bfloat16
    )


def place_kernel(choose_ref, *refs):
    in_refs, (out_hbm, out_ref, sems) = refs[:-3], refs[-3:]
    _, column_vars, parts, share = out_ref.shape
    copies = []
    choose = choose_ref[...]
    wide = [ref[...].astype(jnp.float32) for ref in in_refs]
    for half in range(2):
        rows = slice(half * column_vars, (half + 1) * column_vars)
        stacked = jnp.concatenate([w[rows] for w in wide], axis=0).astype(jnp.bfloat16)
        placed = jnp.dot(choose, stacked, preferred_element_type=jnp.float32)
        out_ref[half] = placed.reshape(column_vars, parts, share).astype(jnp.bfloat16)
        copies.append(pltpu.make_async_copy(out_ref.at[half], out_hbm.at[0, half], sems.at[half]))
        copies[half].start()
    for copy in copies:
        copy.wait()


VMEM_SPEC = pl.BlockSpec(memory_space=pltpu.VMEM)
SMEM_SPEC = pl.BlockSpec(memory_space=pltpu.SMEM)
HBM_SPEC = pl.BlockSpec(memory_space=pltpu.HBM)


def body(cols, bands, adjoint_tend, trajectory, coupling, row_lat, row_points, wave_order):
    column_vars = adjoint_tend.shape[1]
    width = adjoint_tend.shape[3]
    own = trajectory.shape[2]
    waves_total = wave_order.shape[0]
    share = waves_total // bands
    tend = adjoint_tend.reshape(column_vars, width)
    traj = trajectory.reshape(column_vars, own)

    direct = own % LANES == 0 and cols > 2 and cols & (cols - 1) == 0
    across = cols // 2
    swaps = [1, across]
    late_swaps = [2, 3, 5, 7, 6] if cols == 8 else [q for q in range(2, cols) if q != across]
    far = -(-(waves_total - share) // LANES) * LANES
    near = waves_total - (waves_total - share) // LANES * LANES
    blocks = cols if direct else 8
    held = list(reversed(range(bands)))
    block = width // blocks

    def index_of():
        if not direct:
            return list(range(blocks))
        my_col = lax.axis_index("col")
        return [my_col] + [my_col ^ swap for swap in [*swaps, *late_swaps]]

    if direct:
        swapped = lambda x, swap: lax.ppermute(x, "col", [(i, i ^ swap) for i in range(cols)])
        moved = {across: swapped(traj, across)}
        for swap in swaps:
            if swap != across:
                moved[swap] = swapped(traj, swap)
        first = [moved[swap] for swap in swaps]
        pieces = [
            swapped(moved[across], swap ^ across)
            if across < swap < cols - 1
            else swapped(traj, swap)
            for swap in late_swaps
        ]
        early = 1 + len(first)
    else:
        whole = lax.all_gather(traj, "col", axis=1, tiled=True)
        first = []
        pieces = [whole[:, i * block : (i + 1) * block] for i in range(8)]
        early = 0

    operands = [wave_order, coupling, tend, traj]
    far_table, own_table, phase, mix, kept, coriolis, *before = pl.pallas_call(
        functools.partial(tables_kernel, blocks, block, early, held, index_of),
        out_shape=[
            jax.ShapeDtypeStruct((block, 2 * far), jnp.bfloat16),
            jax.ShapeDtypeStruct((block, 2 * near), jnp.bfloat16),
            jax.ShapeDtypeStruct((2, blocks, waves_total), jnp.float32),
            jax.ShapeDtypeStruct((2 * column_vars, 3 * column_vars), jnp.bfloat16),
            jax.ShapeDtypeStruct((column_vars, width), jnp.bfloat16),
            jax.ShapeDtypeStruct((1, LANES), jnp.float32),
        ]
        + [jax.ShapeDtypeStruct((early * column_vars, block), jnp.float32)] * (early > 0),
        in_specs=[SMEM_SPEC] + [HBM_SPEC] * len(operands) + [VMEM_SPEC] * len(first),
        out_specs=[VMEM_SPEC] * (6 + (early > 0)),
        scratch_shapes=[
            pltpu.VMEM((waves_total,), jnp.int32),
            pltpu.VMEM((column_vars, column_vars), jnp.bfloat16),
            pltpu.VMEM((column_vars, width), jnp.bfloat16),
            pltpu.VMEM((column_vars, own), jnp.bfloat16),
            pltpu.SemaphoreType.DMA((len(operands),)),
        ],
        compiler_params=pltpu.CompilerParams(vmem_limit_bytes=16 * 1024 * 1024),
        cost_estimate=pl.CostEstimate(
            flops=1024 * column_vars * width, bytes_accessed=4 * column_vars * width, transcendentals=0
        ),
        name="tables",
    )(row_lat, *[pltpu.with_memory_space_constraint(x, pltpu.HBM) for x in operands], *first)

    spectra = jax.ShapeDtypeStruct((2 * column_vars, share), jnp.bfloat16)
    flat, *parts = pl.pallas_call(
        functools.partial(main_kernel, blocks, block, early, index_of),
        out_shape=[jax.ShapeDtypeStruct((blocks * column_vars, block), jnp.bfloat16)]
        + [spectra] * (bands - 1),
        in_specs=[VMEM_SPEC] * (5 + len(before) + len(pieces)),
        out_specs=[VMEM_SPEC] * bands,
        scratch_shapes=[pltpu.VMEM(((blocks - early) * column_vars, block), jnp.float32)],
        compiler_params=pltpu.CompilerParams(vmem_limit_bytes=24 * 1024 * 1024),
        cost_estimate=pl.CostEstimate(
            flops=4 * column_vars * width * (waves_total - share),
            bytes_accessed=4 * column_vars * width,
            transcendentals=0,
        ),
        name="column_and_waves",
    )(coriolis, mix, far_table, phase, kept, *before, *pieces)
    ready = []
    for step, part in zip(held, parts):
        pairs = [(i, partner(i, step, bands)) for i in range(bands)]
        ready.append(lax.ppermute(part, "band", pairs))
    total = bands * column_vars
    own_part, choose = pl.pallas_call(
        functools.partial(own_kernel, held),
        out_shape=[spectra, jax.ShapeDtypeStruct((total, total), jnp.bfloat16)],
        in_specs=[VMEM_SPEC] * 3,
        out_specs=[VMEM_SPEC] * 2,
        compiler_params=pltpu.CompilerParams(vmem_limit_bytes=24 * 1024 * 1024),
        cost_estimate=pl.CostEstimate(
            flops=4 * column_vars * width * share,
            bytes_accessed=4 * column_vars * width,
            transcendentals=0,
        ),
        name="own_waves",
    )(flat, own_table, phase)
    return pl.pallas_call(
        place_kernel,
        out_shape=jax.ShapeDtypeStruct((1, 2, column_vars, bands, share), jnp.bfloat16),
        in_specs=[VMEM_SPEC] * (1 + bands),
        out_specs=HBM_SPEC,
        scratch_shapes=[
            pltpu.VMEM((2, column_vars, bands, share), jnp.bfloat16),
            pltpu.SemaphoreType.DMA((2,)),
        ],
        compiler_params=pltpu.CompilerParams(vmem_limit_bytes=16 * 1024 * 1024),
        name="row_slots",
    )(choose, *ready, own_part)


def solution(mesh):
    return jax.shard_map(
        functools.partial(body, mesh.shape["col"], mesh.shape["band"]),
        mesh=mesh,
        in_specs=(
            P("col", None, "band", None),
            P(None, "band", "col"),
            P(),
            P("band"),
            P("band"),
            P(),
        ),
        out_specs=P("col", None, None, None, "band"),
        check_vma=False,
    )
```
